32 devices in a mesh: groups: 2 (over x), wide: 16 (over z, y, core).
Axes of the slice: x: 2, y: 2, z: 4, core: 2. Of those that a mesh axis runs over, the one named last changes fastest.
Arguments:
- tokens: bfloat16 [32, 16384], P('groups', 'wide'), parts along dimension 0, may hold values from -6 to 6
- norm_gain: bfloat16 [16384], P('wide'), may hold values from 0.099609375 to 1.8984375
- slot_of_row: int32 [32], P('groups'), parts along dimension 0, may hold values from 0 to 15, each once
- lengths: int32 [32], P('groups'), parts along dimension 0, may hold values from 512 to 4096, as said below
- w_query: bfloat16 [16384, 8192], P(None, 'wide'), may hold values from -1 to 1
- key_projection: bfloat16 [16384, 512], P('wide'), may hold values from -1 to 1
- value_projection: bfloat16 [16384, 512], P('wide'), may hold values from -0.046875 to 0.046875
- output_projection: bfloat16 [8192, 16384], P(None, 'wide'), may hold values from -0.25 to 0.25
- slot_key_cache: bfloat16 [128, 4096, 128], P(('groups', 'wide')), parts along dimension 0, may hold values from -1000 to 1000
- slot_value_cache: bfloat16 [128, 4096, 128], P(('groups', 'wide')), parts along dimension 0, may hold values from -12 to 12
Outputs:
- attn_out: bfloat16 [32, 16384], P('groups', 'wide'), parts along dimension 0
The draws below stay inside these ranges and needn't reach their ends.
There are 2 independent parts, one for each index of `groups`. The reference program is written for one: setup_inputs(seed, part) draws one part's arguments, and reference() takes and returns one part's arrays. A program takes and returns all parts, laid end to end along the dimension named above; an argument that names none is the same for every part. Nothing has to cross between parts.
Inputs may be any that keep to these rules, and one draw needn't show every extreme that they name: `lengths`: at least 512, and 4096 for at least one slot.
All inputs are finite; a program needn't handle non-finite values.
Results may differ from the reference program's by a relative error of at most 0.01.
Values may be sent and summed in bfloat16 or wider, within the bound.
No kernel may reach another device: no remote copies, remote signals or barrier semaphores. Data moves between devices by JAX's collectives and lax.ppermute only.
A program may use at most 128 MiB of HBM per device.

```python
import math
import jax
import jax.numpy as jnp
from jax import lax

MODEL_WIDTH = 16384
QUERY_HEADS = 64
KEY_VALUE_HEADS = 4
HEAD_SIZE = 128
DECODE_ROWS = 16
CACHE_LENGTH = 4096


def shared_query(key):
    base = jnp.clip(jax.random.normal(key, (MODEL_WIDTH, QUERY_HEADS * HEAD_SIZE), jnp.float32), -6.0, 6.0)
    return base * MODEL_WIDTH ** (-0.5)


def draw_w_query(key, part):
    base = shared_query(key)
    return jnp.clip(base, -1.0, 1.0).astype(jnp.bfloat16)


def draw_key_projection(key, part):
    base = shared_query(key)
    key = jax.random.fold_in(key, 23)
    grouped = base.reshape(MODEL_WIDTH, QUERY_HEADS // KEY_VALUE_HEADS, KEY_VALUE_HEADS * HEAD_SIZE)
    centre = jnp.mean(grouped, axis=1)
    noise = jnp.clip(jax.random.normal(key, (MODEL_WIDTH, KEY_VALUE_HEADS * HEAD_SIZE), jnp.float32), -6.0, 6.0) * MODEL_WIDTH ** (-0.5)
    return jnp.clip(12.0 * centre + 0.5 * noise, -1.0, 1.0).astype(jnp.bfloat16)


def draw_lengths(key, part):
    key = jax.random.fold_in(key, 5)
    first_part, second_part = jax.random.split(key)
    spread = jax.random.randint(first_part, (DECODE_ROWS,), CACHE_LENGTH // 8, CACHE_LENGTH + 1)
    chosen = jax.random.randint(second_part, (), 0, DECODE_ROWS)
    return jnp.where(jnp.arange(DECODE_ROWS) == chosen, CACHE_LENGTH, spread).astype(jnp.int32)


def draw_slot_key_cache(key, part):
    key = jax.random.fold_in(key, 11)
    first_part = jax.random.fold_in(key, 0)
    rotary_base = jnp.clip(jax.random.normal(first_part, (KEY_VALUE_HEADS * DECODE_ROWS, CACHE_LENGTH, HEAD_SIZE), jnp.float32), -6.0, 6.0)
    return (1.5 * rotary_base).astype(jnp.bfloat16)


def shard_levels(own_key, extent, cuts, smallest, largest):
    level = 1.0
    for dim, blocks in cuts:
        heights = jax.random.uniform(jax.random.fold_in(jax.random.fold_in(own_key, 6), dim), (blocks,), jnp.float32, smallest / len(cuts), largest / len(cuts))
        level = level * jnp.repeat(jnp.exp(heights), extent[dim] // blocks).reshape((-1,) + (1,) * (len(extent) - 1 - dim))
    return level


def centred(rng, shape, scale, limit, pieces=(), kind=jnp.bfloat16):
    array = scale * jax.random.normal(rng, shape, jnp.float32)
    if pieces:
        array = array * shard_levels(rng, shape, pieces, -0.22, 0.18)
    return jnp.clip(array, -limit, limit).astype(kind)


def setup_inputs(seed: int = 0, part: int = 0) -> dict:
    streams_of = jax.random.split(jax.random.key(seed), 11)
    part_keys = jax.random.split(jax.random.fold_in(streams_of[10], part), 11)
    tokens = centred(part_keys[0], (DECODE_ROWS, MODEL_WIDTH), 1.0, 6.0, ((1, 16),))
    norm_gain = jnp.clip(1.0 + 0.18 * jax.random.normal(streams_of[1], (MODEL_WIDTH,), jnp.float32), 0.099609375, 1.8984375).astype(jnp.bfloat16)
    slot_of_row = jax.random.permutation(part_keys[2], DECODE_ROWS).astype(jnp.int32)
    lengths = draw_lengths(jax.random.fold_in(jax.random.fold_in(streams_of[10], part), 71), part)
    w_query = draw_w_query(jax.random.fold_in(streams_of[10], 71), part)
    key_projection = draw_key_projection(jax.random.fold_in(streams_of[10], 71), part)
    value_projection = centred(streams_of[6], (MODEL_WIDTH, KEY_VALUE_HEADS * HEAD_SIZE), MODEL_WIDTH ** -0.5, 0.046875, ((0, 16),))
    output_projection = centred(streams_of[7], (QUERY_HEADS * HEAD_SIZE, MODEL_WIDTH), (QUERY_HEADS * HEAD_SIZE // 16) ** -0.5, 0.25, ((1, 16),))
    slot_key_cache = draw_slot_key_cache(jax.random.fold_in(jax.random.fold_in(streams_of[10], part), 71), part)
    slot_value_cache = centred(part_keys[9], (KEY_VALUE_HEADS * DECODE_ROWS, CACHE_LENGTH, HEAD_SIZE), 2.0, 12.0, ((0, 16),))
    return dict(tokens=tokens, norm_gain=norm_gain, slot_of_row=slot_of_row, lengths=lengths, w_query=w_query, key_projection=key_projection, value_projection=value_projection, output_projection=output_projection, slot_key_cache=slot_key_cache, slot_value_cache=slot_value_cache)


EPS = 1e-05
ROPE_BASE = 500000.0

def rotate(mat, positions, start):
    rows, cols = mat.shape
    index = (start + jnp.arange(cols, dtype=jnp.int32)) % HEAD_SIZE
    rate = ROPE_BASE ** (-(index - index % 2).astype(jnp.float32) / HEAD_SIZE)
    angle = positions.astype(jnp.float32)[:, None] * rate[None, :]
    paired = mat.reshape(rows, cols // 2, 2)
    swapped = jnp.stack([-paired[..., 1], paired[..., 0]], axis=-1).reshape(rows, cols)
    return mat * jnp.cos(angle) + swapped * jnp.sin(angle)

def reference(tokens, norm_gain, slot_of_row, lengths, w_query, key_projection, value_projection, output_projection, slot_key_cache, slot_value_cache):
    query_group = QUERY_HEADS // KEY_VALUE_HEADS
    score_scale = 1.0 / math.sqrt(HEAD_SIZE)
    wide_f = tokens.astype(jnp.float32)
    normed = (wide_f * lax.rsqrt(lax.optimization_barrier(jnp.mean(wide_f * wide_f, axis=1, keepdims=True)) + EPS) * norm_gain.astype(jnp.float32)).astype(jnp.bfloat16)
    positions = lengths[slot_of_row]
    query_vector = rotate(jnp.dot(normed, w_query, preferred_element_type=jnp.float32), positions, 0).astype(jnp.bfloat16)
    fresh_key = rotate(jnp.dot(normed, key_projection, preferred_element_type=jnp.float32), positions, 0).astype(jnp.bfloat16)
    fresh_value = jnp.dot(normed, value_projection, preferred_element_type=jnp.float32).astype(jnp.bfloat16)
    slot_row_lookup = jnp.zeros((DECODE_ROWS,), jnp.int32).at[slot_of_row].set(jnp.arange(DECODE_ROWS, dtype=jnp.int32))
    query_slot_rows = query_vector[slot_row_lookup].reshape(DECODE_ROWS, query_group, KEY_VALUE_HEADS, HEAD_SIZE).transpose(2, 0, 1, 3)
    key_slot_rows = fresh_key[slot_row_lookup].reshape(DECODE_ROWS, KEY_VALUE_HEADS, HEAD_SIZE).transpose(1, 0, 2)
    value_slot_rows = fresh_value[slot_row_lookup].reshape(DECODE_ROWS, KEY_VALUE_HEADS, HEAD_SIZE).transpose(1, 0, 2)
    key_rows = slot_key_cache.reshape(KEY_VALUE_HEADS, DECODE_ROWS, CACHE_LENGTH, HEAD_SIZE)
    value_rows = slot_value_cache.reshape(KEY_VALUE_HEADS, DECODE_ROWS, CACHE_LENGTH, HEAD_SIZE)

    def one_head(items):
        q_h, k_h, v_h, cached_key_rows, cached_value_rows = items
        query_float = q_h.astype(jnp.float32)
        logit_scores = jnp.einsum('oqx,ofx->oqf', query_float, cached_key_rows.astype(jnp.float32)) * score_scale
        valid = jnp.arange(CACHE_LENGTH)[None, None, :] < lengths[:, None, None]
        own = lax.optimization_barrier(jnp.sum(query_float * k_h.astype(jnp.float32)[:, None, :], axis=-1)) * score_scale
        top = jnp.maximum(lax.optimization_barrier(jnp.max(jnp.where(valid, logit_scores, -jnp.inf), axis=-1)), own)
        weights = jnp.where(valid, jnp.exp(logit_scores - top[..., None]), 0.0)
        own_w = jnp.exp(own - top)
        denom = lax.optimization_barrier(jnp.sum(weights, axis=-1)) + own_w
        attention_probability = (weights / denom[..., None]).astype(jnp.bfloat16)
        own_p = (own_w / denom).astype(jnp.bfloat16)
        blended_values = jnp.einsum('yku,yuw->ykw', attention_probability.astype(jnp.float32), cached_value_rows.astype(jnp.float32))
        blended_values = blended_values + own_p.astype(jnp.float32)[..., None] * v_h.astype(jnp.float32)[:, None, :]
        return blended_values.astype(jnp.bfloat16)
    attended = lax.map(one_head, (query_slot_rows, key_slot_rows, value_slot_rows, key_rows, value_rows))
    by_slot = attended.transpose(1, 2, 0, 3).reshape(DECODE_ROWS, QUERY_HEADS * HEAD_SIZE)
    by_row = by_slot[slot_of_row]
    return jnp.dot(by_row, output_projection, preferred_element_type=jnp.float32).astype(jnp.bfloat16)
```

```python
import functools
import math

import jax
import jax.numpy as jnp
from jax import lax
from jax.experimental import pallas as pl
from jax.experimental.pallas import tpu as pltpu
from jax.sharding import PartitionSpec as P

QUERY_HEADS = 64
KEY_VALUE_HEADS = 4
HEAD_SIZE = 128
QUERY_GROUP = QUERY_HEADS // KEY_VALUE_HEADS

EPS = 1e-05
ROPE_BASE = 500000.0
MIB = 1 << 20
F32 = jnp.float32
BF16 = jnp.bfloat16


def call(kernel, out_shape, args, near=(), smem=(), scratch=(), limit=4 * MIB, flops=0, read=0):
    operands, specs = [], []
    for i, arg in enumerate(args):
        if i in near:
            arg = pltpu.with_memory_space_constraint(arg, pltpu.VMEM)
        operands.append(arg)
        specs.append(pl.BlockSpec(memory_space=pltpu.SMEM if i in smem else pltpu.VMEM))
    return pl.pallas_call(
        kernel,
        out_shape=out_shape,
        in_specs=specs,
        out_specs=jax.tree.map(lambda _: pl.BlockSpec(memory_space=pltpu.VMEM), out_shape),
        scratch_shapes=list(scratch),
        compiler_params=pltpu.CompilerParams(vmem_limit_bytes=limit),
        cost_estimate=pl.CostEstimate(flops=flops, bytes_accessed=read, transcendentals=0),
    )(*operands)


def prepare_kernel(tokens_ref, gain_ref, slot_ref, scaled_ref, squares_ref):
    rows = tokens_ref.shape[0]
    wide_f = tokens_ref[...].astype(F32)
    squares = jnp.sum(wide_f * wide_f, axis=1, keepdims=True)
    scaled = (wide_f * gain_ref[...].astype(F32)).astype(BF16)
    picked = lax.broadcasted_iota(jnp.int32, (rows, rows), 0) == slot_ref[...]
    scaled_ref[...] = jnp.dot(
        picked.astype(BF16), scaled, preferred_element_type=F32
    ).astype(BF16)
    turned = jnp.sum(jnp.where(picked, jnp.transpose(jnp.broadcast_to(squares, (rows, rows))), 0.0), axis=1, keepdims=True)
    squares_ref[...] = jnp.broadcast_to(turned, squares_ref.shape)


def share_kernel(scaled_ref, key_ref, value_ref, key_share_ref, value_share_ref):
    key_share_ref[...] = jnp.dot(scaled_ref[...], key_ref[...], preferred_element_type=F32)
    value_share_ref[...] = jnp.dot(scaled_ref[...], value_ref[...], preferred_element_type=F32)


def add_blocks(offsets, place, blocks_ref, weight_ref, total):
    features = blocks_ref.shape[2]
    for k, offset in enumerate(offsets):
        start = pl.multiple_of((place ^ offset) * features, features)
        total = total + jnp.dot(
            blocks_ref[k], weight_ref[pl.ds(start, features), :], preferred_element_type=F32
        )
    return total


def query_kernel(offsets, place_ref, blocks_ref, weight_ref, *rest):
    total = rest[0][...] if len(rest) > 1 else jnp.zeros(rest[-1].shape, F32)
    rest[-1][...] = add_blocks(offsets, place_ref[0], blocks_ref, weight_ref, total)


def message_kernel(
    offsets, pairs, place_ref, blocks_ref, weight_ref, total_ref, key_ref, value_ref, squares_ref, message_ref
):
    query = add_blocks(offsets, place_ref[0], blocks_ref, weight_ref, total_ref[...])
    rows = query.shape[0]
    held = query.shape[1] // HEAD_SIZE
    for target in range(message_ref.shape[0]):
        head, first = target * pairs // rows, target * pairs % rows
        slots = slice(first, first + pairs)
        columns = slice(head * HEAD_SIZE, (head + 1) * HEAD_SIZE)
        sent = range(head, held, KEY_VALUE_HEADS) if held % KEY_VALUE_HEADS == 0 else range(held)
        at = 0
        for j in sent:
            message_ref[target, at : at + pairs, :] = query[slots, j * HEAD_SIZE : (j + 1) * HEAD_SIZE]
            at += pairs
        message_ref[target, at : at + pairs, :] = key_ref[slots, columns]
        message_ref[target, at + pairs : at + 2 * pairs, :] = value_ref[slots, columns]
        message_ref[target, at + 2 * pairs : at + 3 * pairs, :] = squares_ref[slots, :]


def rotated(values, cosines, sines):
    even = lax.broadcasted_iota(jnp.int32, values.shape, 1) % 2 == 0
    swapped = jnp.where(
        even, -pltpu.roll(values, HEAD_SIZE - 1, 1), pltpu.roll(values, 1, 1)
    )
    return values * cosines + swapped * sines


def attend_kernel(
    pairs, width, lengths_ref, query_ref, rest_ref, cos_ref, sin_ref, keys_ref, values_ref, out_ref, wide_ref
):
    group = query_ref.shape[0]
    at = rest_ref.shape[1] - 3 * pairs
    summed = jnp.sum(rest_ref[:, at:, :], axis=0)
    score_scale = 1.0 / math.sqrt(HEAD_SIZE)
    for i in range(pairs):
        length = lengths_ref[i]
        scale = lax.rsqrt(summed[2 * pairs + i : 2 * pairs + i + 1, :] * (1.0 / width) + EPS)
        cosines, sines = cos_ref[i : i + 1, :], sin_ref[i : i + 1, :]
        query = rotated(query_ref[:, i, :] * scale, cosines, sines).astype(BF16)
        key = jnp.broadcast_to(summed[i : i + 1, :] * scale, (8, HEAD_SIZE))
        key = rotated(key, cosines, sines)[0:1, :].astype(BF16).astype(F32)
        value = (summed[pairs + i : pairs + i + 1, :] * scale).astype(BF16).astype(F32)
        own = jnp.sum(query.astype(F32) * key, axis=1, keepdims=True) * score_scale
        scores = (
            lax.dot_general(
                query, keys_ref[i], (((1,), (1,)), ((), ())), preferred_element_type=F32
            )
            * score_scale
        )
        valid = lax.broadcasted_iota(jnp.int32, scores.shape, 1) < length
        scores = jnp.where(valid, scores, -jnp.inf)
        top = jnp.maximum(jnp.max(scores, axis=1, keepdims=True), own)
        weights = jnp.exp(scores - top)
        own_w = jnp.exp(own - top)
        share = 1.0 / (jnp.sum(weights, axis=1, keepdims=True) + own_w)
        own_p = (own_w * share).astype(BF16).astype(F32)
        blended = (
            jnp.dot((weights * share).astype(BF16), values_ref[i], preferred_element_type=F32)
            + own_p * value
        )
        for g in range(group):
            wide_ref[i : i + 1, g * HEAD_SIZE : (g + 1) * HEAD_SIZE] = blended[g : g + 1, :]
    out_ref[...] = wide_ref[...].astype(BF16)


def project_kernel(
    pairs, head_offsets, slot_offsets, place_ref, slot_ref, mine_ref, other_ref, weight_ref, out_ref, left_ref
):
    heads, half, _ = mine_ref.shape
    rows, columns = out_ref.shape
    devices_of_head = rows // pairs
    group_place = place_ref[0] % devices_of_head
    head_place = place_ref[0] // devices_of_head
    position = lax.broadcasted_iota(jnp.int32, (rows, half), 1)

    def picked(offsets):
        device = jnp.zeros_like(position)
        for k, offset in enumerate(offsets):
            device = jnp.where(position // pairs == k, group_place ^ offset, device)
        return (slot_ref[...] == device * pairs + position % pairs).astype(BF16)

    mine_pick, other_pick = picked(slot_offsets[: half // pairs]), picked(slot_offsets[half // pairs :])
    for z, offset in enumerate(head_offsets):
        head = head_place ^ offset
        ordered = (
            jnp.dot(mine_pick, mine_ref[z], preferred_element_type=F32)
            + jnp.dot(other_pick, other_ref[z], preferred_element_type=F32)
        ).astype(BF16)
        for g in range(QUERY_GROUP):
            start = pl.multiple_of((g * heads + head) * HEAD_SIZE, HEAD_SIZE)
            left_ref[:, pl.ds(start, HEAD_SIZE)] = ordered[:, g * HEAD_SIZE : (g + 1) * HEAD_SIZE]
    depth = weight_ref.shape[0]
    step = min(1024, depth)

    def add(k, total):
        at = pl.multiple_of(k * step, step)
        return total + jnp.dot(
            left_ref[:, pl.ds(at, step)], weight_ref[pl.ds(at, step), :], preferred_element_type=F32
        )

    total = lax.fori_loop(0, depth // step, add, jnp.zeros((rows, columns), F32))
    out_ref[...] = total.astype(BF16)


def swap(array, bit, count):
    return lax.ppermute(array, "wide", [(i, i ^ bit) for i in range(count)])


def body(
    count,
    tokens,
    norm_gain,
    slot_of_row,
    lengths,
    w_query,
    key_projection,
    value_projection,
    output_projection,
    slot_key_cache,
    slot_value_cache,
):
    place = lax.axis_index("wide")
    rows, features = tokens.shape
    pairs = slot_key_cache.shape[0]
    width = w_query.shape[0]
    query_columns = w_query.shape[1]
    held = query_columns // HEAD_SIZE
    devices_of_head = rows // pairs
    bits = [1 << b for b in reversed(range(count.bit_length() - 1))]
    places = place.astype(jnp.int32).reshape(1)

    scaled, squares = call(
        prepare_kernel,
        (
            jax.ShapeDtypeStruct((rows, features), BF16),
            jax.ShapeDtypeStruct((rows, HEAD_SIZE), F32),
        ),
        (tokens, norm_gain.reshape(1, features), slot_of_row.reshape(1, rows)),
    )
    shares = jax.ShapeDtypeStruct((rows, key_projection.shape[1]), F32)
    key_share, value_share = call(
        share_kernel,
        (shares, shares),
        (scaled, key_projection, value_projection),
        near=(1, 2),
        flops=4 * rows * key_projection.size,
        read=4 * key_projection.size,
    )

    blocks, offsets, total = scaled[None], [0], None
    done = 0
    for bit in bits:
        arrived = swap(blocks, bit, count)
        if len(offsets) - done >= 4 or bit == 1:
            part = blocks[done:]
            total = call(
                functools.partial(query_kernel, tuple(offsets[done:])),
                jax.ShapeDtypeStruct((rows, query_columns), F32),
                (places, part, w_query) + (() if total is None else (total,)),
                near=(1, 2),
                smem=(0,),
                flops=2 * part.size * query_columns,
                read=2 * part.shape[0] * features * query_columns,
            )
            done = len(offsets)
        if bit > 1:
            blocks = jnp.concatenate([blocks, arrived], 0)
        offsets = offsets + [o ^ bit for o in offsets]
    half = count // 2
    sent = held // KEY_VALUE_HEADS if held % KEY_VALUE_HEADS == 0 else held
    message = call(
        functools.partial(message_kernel, tuple(offsets[half:]), pairs),
        jax.ShapeDtypeStruct((count, pairs * (sent + 3), HEAD_SIZE), F32),
        (places, arrived, w_query, total, key_share, value_share, squares),
        near=(1, 2),
        smem=(0,),
        flops=2 * arrived.size * query_columns,
        read=2 * half * features * query_columns,
    )

    got = lax.all_to_all(message, "wide", 0, 0, tiled=True)
    if sent == 1 and held % KEY_VALUE_HEADS == 0:
        query_rows = got
    else:
        query_rows = (
            got[:, : pairs * sent].reshape(count, sent, pairs, HEAD_SIZE).reshape(-1, pairs, HEAD_SIZE)
        )
        if held % KEY_VALUE_HEADS:
            head = place // devices_of_head
            query_rows = lax.dynamic_index_in_dim(
                query_rows.reshape(QUERY_GROUP, KEY_VALUE_HEADS, pairs, HEAD_SIZE), head, 1, False
            )
    first = (place * pairs) % rows
    own_lengths = lax.dynamic_slice_in_dim(lengths, first, pairs, 0)
    index = jnp.arange(HEAD_SIZE, dtype=jnp.int32)
    rate = ROPE_BASE ** (-(index - index % 2).astype(F32) / HEAD_SIZE)
    angle = own_lengths.astype(F32)[:, None] * rate[None, :]
    cache_bytes = 2 * slot_key_cache.size
    attended = call(
        functools.partial(attend_kernel, pairs, width),
        jax.ShapeDtypeStruct((pairs, QUERY_GROUP * HEAD_SIZE), BF16),
        (own_lengths, query_rows, got, jnp.cos(angle), jnp.sin(angle), slot_key_cache, slot_value_cache),
        near=(5, 6),
        smem=(0,),
        scratch=(pltpu.VMEM((pairs, QUERY_GROUP * HEAD_SIZE), F32),),
        limit=8 * MIB,
        flops=4 * QUERY_GROUP * slot_key_cache.size,
        read=2 * cache_bytes,
    )

    mine = attended[None]
    for bit in bits:
        other = swap(mine, bit, count)
        if bit > 1:
            mine = jnp.concatenate([mine, other], 0 if bit >= devices_of_head else 1)
    head_offsets, slot_offsets = [0], [0]
    for bit in bits:
        if bit >= devices_of_head:
            head_offsets = head_offsets + [o ^ (bit // devices_of_head) for o in head_offsets]
        else:
            slot_offsets = slot_offsets + [o ^ bit for o in slot_offsets]
    return call(
        functools.partial(project_kernel, pairs, tuple(head_offsets), tuple(slot_offsets)),
        jax.ShapeDtypeStruct((rows, output_projection.shape[1]), BF16),
        (places, slot_of_row.reshape(rows, 1), mine, other, output_projection),
        near=(4,),
        smem=(0,),
        scratch=(pltpu.VMEM((rows, output_projection.shape[0]), BF16),),
        flops=2 * rows * output_projection.size,
        read=2 * output_projection.size,
    )


def solution(mesh):
    placed = (
        P("groups", "wide"),
        P("wide"),
        P("groups"),
        P("groups"),
        P(None, "wide"),
        P("wide", None),
        P("wide", None),
        P(None, "wide"),
        P(("groups", "wide"), None, None),
        P(("groups", "wide"), None, None),
    )
    return jax.shard_map(
        functools.partial(body, mesh.shape["wide"]),
        mesh=mesh,
        in_specs=placed,
        out_specs=P("groups", "wide"),
        check_vma=False,
    )
```

```python
import functools
import math

import jax
import jax.numpy as jnp
import numpy as np
from jax import lax
from jax.experimental import pallas as pl
from jax.experimental.pallas import tpu as pltpu
from jax.sharding import PartitionSpec as P

QUERY_HEADS = 64
KEY_VALUE_HEADS = 4
HEAD_SIZE = 128
QUERY_GROUP = QUERY_HEADS // KEY_VALUE_HEADS

EPS = 1e-05
ROPE_BASE = 500000.0
MIB = 1 << 20
F32 = jnp.float32
BF16 = jnp.bfloat16


def call(kernel, out_shape, args, near=(), far=(), smem=(), scratch=(), limit=4 * MIB, flops=0, read=0):
    operands, specs = [], []
    for i, arg in enumerate(args):
        space = pltpu.SMEM if i in smem else pltpu.VMEM
        if i in near:
            arg = pltpu.with_memory_space_constraint(arg, pltpu.VMEM)
        if i in far:
            arg = pltpu.with_memory_space_constraint(arg, pltpu.HBM)
            space = pltpu.HBM
        operands.append(arg)
        specs.append(pl.BlockSpec(memory_space=space))
    return pl.pallas_call(
        kernel,
        out_shape=out_shape,
        in_specs=specs,
        out_specs=jax.tree.map(lambda _: pl.BlockSpec(memory_space=pltpu.VMEM), out_shape),
        scratch_shapes=list(scratch),
        compiler_params=pltpu.CompilerParams(vmem_limit_bytes=limit),
        cost_estimate=pl.CostEstimate(flops=flops, bytes_accessed=read, transcendentals=0),
    )(*operands)


def prepare_kernel(far_tokens, far_gain, far_slot, scaled_ref, squares_ref, tokens_ref, gain_ref, slot_ref, sems):
    copies = [
        pltpu.make_async_copy(far, near, sems.at[i])
        for i, (far, near) in enumerate(
            ((far_tokens, tokens_ref), (far_gain, gain_ref), (far_slot, slot_ref))
        )
    ]
    for copy in copies:
        copy.start()
    for copy in copies:
        copy.wait()
    rows, features = tokens_ref.shape
    wide_f = tokens_ref[...].astype(F32)
    squares = jnp.sum(wide_f * wide_f, axis=1, keepdims=True)
    gain = gain_ref[...].astype(F32).reshape(1, features)
    scaled = (wide_f * gain).astype(BF16)
    picked = lax.broadcasted_iota(jnp.int32, (rows, rows), 0) == slot_ref[...]
    scaled_ref[...] = jnp.dot(
        picked.astype(BF16), scaled, preferred_element_type=F32
    ).astype(BF16)
    turned = jnp.sum(jnp.where(picked, jnp.transpose(jnp.broadcast_to(squares, (rows, rows))), 0.0), axis=1, keepdims=True)
    squares_ref[...] = jnp.broadcast_to(turned, squares_ref.shape)


def join_kernel(mine_ref, arrived_ref, after_ref, joined_ref):
    count = mine_ref.shape[0]
    joined_ref[:count] = mine_ref[...]
    joined_ref[count:] = arrived_ref[...]


def weight_rows(place, offset, features, weight_ref):
    return weight_ref.at[pl.ds(pl.multiple_of((place ^ offset) * features, features), features), :]


def window_kernel(offsets, ahead, shares, blocks_ref, weight_ref, *refs):
    refs = list(refs)
    key_ref, value_ref = (refs.pop(0), refs.pop(0)) if shares else (None, None)
    total_in = None if shares else refs.pop(0)
    total_ref = refs.pop(0)
    key_share_ref, value_share_ref = (refs.pop(0), refs.pop(0)) if shares else (None, None)
    ahead_ref = refs.pop(0) if ahead else None
    held_ref, sems = refs.pop(0), refs.pop(0)
    features = blocks_ref.shape[2]
    place = lax.axis_index("wide")
    copies = []
    if shares:
        near_key, near_value = refs
        copies += [
            pltpu.make_async_copy(key_ref, near_key, sems.at[0]),
            pltpu.make_async_copy(value_ref, near_value, sems.at[1]),
        ]
    for k, offset in enumerate(offsets):
        copies.append(
            pltpu.make_async_copy(
                weight_rows(place, offset, features, weight_ref), held_ref.at[k], sems.at[len(copies)]
            )
        )
    fetched = []
    for k, offset in enumerate(ahead):
        fetched.append(
            pltpu.make_async_copy(
                weight_rows(place, offset, features, weight_ref),
                ahead_ref.at[k],
                sems.at[len(copies) + len(fetched)],
            )
        )
    for copy in copies + fetched:
        copy.start()
    first = blocks_ref.shape[0] - len(offsets)
    if shares:
        copies[0].wait()
        key_share_ref[...] = jnp.dot(blocks_ref[0], near_key[...], preferred_element_type=F32)
        copies[1].wait()
        value_share_ref[...] = jnp.dot(blocks_ref[0], near_value[...], preferred_element_type=F32)
        copies = copies[2:]
    total = jnp.zeros(total_ref.shape, F32) if total_in is None else total_in[...]
    for k, copy in enumerate(copies):
        copy.wait()
        total = total + jnp.dot(blocks_ref[first + k], held_ref[k], preferred_element_type=F32)
    total_ref[...] = total
    for copy in fetched:
        copy.wait()


def message_kernel(
    pairs, blocks_ref, total_ref, key_ref, value_ref, squares_ref, *refs
):
    message_ref = refs[-1]
    query, block = total_ref[...], 0
    for weight_ref in refs[:-1]:
        for k in range(weight_ref.shape[0]):
            query = query + jnp.dot(blocks_ref[block], weight_ref[k], preferred_element_type=F32)
            block += 1
    rows = query.shape[0]
    held = query.shape[1] // HEAD_SIZE
    for target in range(message_ref.shape[0]):
        head, first = target * pairs // rows, target * pairs % rows
        slots = slice(first, first + pairs)
        columns = slice(head * HEAD_SIZE, (head + 1) * HEAD_SIZE)
        sent = range(head, held, KEY_VALUE_HEADS) if held % KEY_VALUE_HEADS == 0 else range(held)
        at = 0
        for j in sent:
            message_ref[target, at : at + pairs, :] = query[slots, j * HEAD_SIZE : (j + 1) * HEAD_SIZE]
            at += pairs
        message_ref[target, at : at + pairs, :] = key_ref[slots, columns]
        message_ref[target, at + pairs : at + 2 * pairs, :] = value_ref[slots, columns]
        message_ref[target, at + 2 * pairs : at + 3 * pairs, :] = squares_ref[slots, :]


def rotated(values, cosines, sines):
    even = lax.broadcasted_iota(jnp.int32, values.shape, 1) % 2 == 0
    swapped = jnp.where(
        even, -pltpu.roll(values, HEAD_SIZE - 1, 1), pltpu.roll(values, 1, 1)
    )
    return values * cosines + swapped * sines


def attend_kernel(
    pairs, width, lengths_ref, rate_ref, query_ref, rest_ref, keys_ref, values_ref, out_ref, wide_ref
):
    group = query_ref.shape[0]
    first = (lax.axis_index("wide") * pairs) % lengths_ref.shape[0]
    positions = jnp.concatenate(
        [jnp.full((1, HEAD_SIZE), lengths_ref[first + i], jnp.int32) for i in range(pairs)], 0
    )
    angle = positions.astype(F32) * rate_ref[...]
    all_cosines, all_sines = jnp.cos(angle), jnp.sin(angle)
    at = rest_ref.shape[1] - 3 * pairs
    summed = jnp.sum(rest_ref[:, at:, :], axis=0)
    score_scale = 1.0 / math.sqrt(HEAD_SIZE)
    for i in range(pairs):
        length = lengths_ref[first + i]
        scale = lax.rsqrt(summed[2 * pairs + i : 2 * pairs + i + 1, :] * (1.0 / width) + EPS)
        cosines, sines = all_cosines[i : i + 1, :], all_sines[i : i + 1, :]
        query = rotated(query_ref[:, i, :] * scale, cosines, sines).astype(BF16)
        key = jnp.broadcast_to(summed[i : i + 1, :] * scale, (8, HEAD_SIZE))
        key = rotated(key, cosines, sines)[0:1, :].astype(BF16).astype(F32)
        value = (summed[pairs + i : pairs + i + 1, :] * scale).astype(BF16).astype(F32)
        own = jnp.sum(query.astype(F32) * key, axis=1, keepdims=True) * score_scale
        scores = (
            lax.dot_general(
                query, keys_ref[i], (((1,), (1,)), ((), ())), preferred_element_type=F32
            )
            * score_scale
        )
        valid = lax.broadcasted_iota(jnp.int32, scores.shape, 1) < length
        scores = jnp.where(valid, scores, -jnp.inf)
        top = jnp.maximum(jnp.max(scores, axis=1, keepdims=True), own)
        weights = jnp.exp(scores - top)
        own_w = jnp.exp(own - top)
        share = 1.0 / (jnp.sum(weights, axis=1, keepdims=True) + own_w)
        own_p = (own_w * share).astype(BF16).astype(F32)
        blended = (
            jnp.dot((weights * share).astype(BF16), values_ref[i], preferred_element_type=F32)
            + own_p * value
        )
        for g in range(group):
            wide_ref[i : i + 1, g * HEAD_SIZE : (g + 1) * HEAD_SIZE] = blended[g : g + 1, :]
    out_ref[...] = wide_ref[...].astype(BF16)


def project_kernel(
    pairs, head_offsets, slot_offsets, slot_ref, mine_ref, other_ref, weight_ref, out_ref, left_ref
):
    heads, half, _ = mine_ref.shape
    rows, columns = out_ref.shape
    devices_of_head = rows // pairs
    place = lax.axis_index("wide")
    group_place = place % devices_of_head
    head_place = place // devices_of_head
    slot_of_row = jnp.transpose(jnp.broadcast_to(slot_ref[...], (rows, rows)))[:, 0:1]
    position = lax.broadcasted_iota(jnp.int32, (rows, half), 1)

    def picked(offsets):
        device = jnp.zeros_like(position)
        for k, offset in enumerate(offsets):
            device = jnp.where(position // pairs == k, group_place ^ offset, device)
        return (slot_of_row == device * pairs + position % pairs).astype(BF16)

    mine_pick, other_pick = picked(slot_offsets[: half // pairs]), picked(slot_offsets[half // pairs :])
    for z, offset in enumerate(head_offsets):
        head = head_place ^ offset
        ordered = (
            jnp.dot(mine_pick, mine_ref[z], preferred_element_type=F32)
            + jnp.dot(other_pick, other_ref[z], preferred_element_type=F32)
        ).astype(BF16)
        for g in range(QUERY_GROUP):
            start = pl.multiple_of((g * heads + head) * HEAD_SIZE, HEAD_SIZE)
            left_ref[:, pl.ds(start, HEAD_SIZE)] = ordered[:, g * HEAD_SIZE : (g + 1) * HEAD_SIZE]
    depth = weight_ref.shape[0]
    step = min(1024, depth)

    def add(k, total):
        at = pl.multiple_of(k * step, step)
        return total + jnp.dot(
            left_ref[:, pl.ds(at, step)], weight_ref[pl.ds(at, step), :], preferred_element_type=F32
        )

    total = lax.fori_loop(0, depth // step, add, jnp.zeros((rows, columns), F32))
    out_ref[...] = total.astype(BF16)


def swap(array, bit, count):
    return lax.ppermute(array, "wide", [(i, i ^ bit) for i in range(count)])


def body(
    count,
    tokens,
    norm_gain,
    slot_of_row,
    lengths,
    w_query,
    key_projection,
    value_projection,
    output_projection,
    slot_key_cache,
    slot_value_cache,
):
    rows, features = tokens.shape
    pairs = slot_key_cache.shape[0]
    width = w_query.shape[0]
    query_columns = w_query.shape[1]
    held = query_columns // HEAD_SIZE
    devices_of_head = rows // pairs
    bits = [1 << b for b in reversed(range(count.bit_length() - 1))]

    scaled, squares = call(
        prepare_kernel,
        (
            jax.ShapeDtypeStruct((rows, features), BF16),
            jax.ShapeDtypeStruct((rows, HEAD_SIZE), F32),
        ),
        (tokens, norm_gain, slot_of_row.reshape(1, rows)),
        far=(0, 1, 2),
        scratch=(
            pltpu.VMEM((rows, features), BF16),
            pltpu.VMEM((features,), BF16),
            pltpu.VMEM((1, rows), jnp.int32),
            pltpu.SemaphoreType.DMA((3,)),
        ),
    )

    half = count // 2
    last = [0]
    for bit in bits[:-1]:
        last = last + [o ^ bit for o in last]
    last = [o ^ bits[-1] for o in last]
    cuts = [0, half // 4, 3 * half // 4, half]
    block_bytes = 2 * features * query_columns
    totals = jax.ShapeDtypeStruct((rows, query_columns), F32)
    shares = jax.ShapeDtypeStruct((rows, key_projection.shape[1]), F32)
    blocks, offsets, new, total, fetched = scaled[None], [0], [0], None, []
    for step, bit in enumerate(bits):
        arrived = swap(blocks, bit, count)
        ahead = tuple(last[cuts[step] : cuts[step + 1]]) if step < 3 else ()
        outs, args, scratch = [totals], [blocks, w_query], []
        if step == 0:
            outs += [shares, shares]
            args += [key_projection, value_projection]
            scratch = [pltpu.VMEM(key_projection.shape, BF16), pltpu.VMEM(value_projection.shape, BF16)]
        else:
            args.append(total)
        if ahead:
            outs.append(pltpu.VMEM((len(ahead), features, query_columns), BF16))
        got = call(
            functools.partial(window_kernel, tuple(new), ahead, step == 0),
            tuple(outs),
            tuple(args),
            near=(0,),
            far=(1, 2, 3) if step == 0 else (1,),
            scratch=[
                pltpu.VMEM((len(new), features, query_columns), BF16),
                pltpu.SemaphoreType.DMA((len(new) + len(ahead) + 2,)),
                *scratch,
            ],
            limit=8 * MIB,
            flops=2 * rows * len(new) * features * query_columns,
            read=(len(new) + len(ahead)) * block_bytes,
        )
        total = got[0]
        if step == 0:
            key_share, value_share = got[1:3]
        if ahead:
            fetched.append(got[-1])
        if bit > 1:
            blocks = call(
                join_kernel,
                jax.ShapeDtypeStruct((2 * len(offsets), rows, features), BF16),
                (blocks, arrived, total),
            )
        new = [o ^ bit for o in offsets]
        offsets = offsets + new
    sent = held // KEY_VALUE_HEADS if held % KEY_VALUE_HEADS == 0 else held
    message = call(
        functools.partial(message_kernel, pairs),
        jax.ShapeDtypeStruct((count, pairs * (sent + 3), HEAD_SIZE), F32),
        (arrived, total, key_share, value_share, squares, *fetched),
        near=(0, *range(5, 5 + len(fetched))),
        flops=2 * arrived.size * query_columns,
        read=half * block_bytes,
    )

    got = lax.all_to_all(message, "wide", 0, 0, tiled=True)
    if sent == 1 and held % KEY_VALUE_HEADS == 0:
        query_rows = got
    else:
        query_rows = (
            got[:, : pairs * sent].reshape(count, sent, pairs, HEAD_SIZE).reshape(-1, pairs, HEAD_SIZE)
        )
        if held % KEY_VALUE_HEADS:
            head = lax.axis_index("wide") // devices_of_head
            query_rows = lax.dynamic_index_in_dim(
                query_rows.reshape(QUERY_GROUP, KEY_VALUE_HEADS, pairs, HEAD_SIZE), head, 1, False
            )
    index = np.arange(HEAD_SIZE)
    rate = (ROPE_BASE ** (-(index - index % 2) / HEAD_SIZE)).astype(np.float32)[None, :]
    cache_bytes = 2 * slot_key_cache.size
    attended = call(
        functools.partial(attend_kernel, pairs, width),
        jax.ShapeDtypeStruct((pairs, QUERY_GROUP * HEAD_SIZE), BF16),
        (lengths, jnp.asarray(rate), query_rows, got, slot_key_cache, slot_value_cache),
        near=(4, 5),
        smem=(0,),
        scratch=(pltpu.VMEM((pairs, QUERY_GROUP * HEAD_SIZE), F32),),
        limit=8 * MIB,
        flops=4 * QUERY_GROUP * slot_key_cache.size,
        read=2 * cache_bytes,
    )

    mine = attended[None]
    for bit in bits:
        other = swap(mine, bit, count)
        if bit > 1:
            mine = jnp.concatenate([mine, other], 0 if bit >= devices_of_head else 1)
    head_offsets, slot_offsets = [0], [0]
    for bit in bits:
        if bit >= devices_of_head:
            head_offsets = head_offsets + [o ^ (bit // devices_of_head) for o in head_offsets]
        else:
            slot_offsets = slot_offsets + [o ^ bit for o in slot_offsets]
    return call(
        functools.partial(project_kernel, pairs, tuple(head_offsets), tuple(slot_offsets)),
        jax.ShapeDtypeStruct((rows, output_projection.shape[1]), BF16),
        (slot_of_row.reshape(1, rows), mine, other, output_projection),
        near=(3,),
        scratch=(pltpu.VMEM((rows, output_projection.shape[0]), BF16),),
        flops=2 * rows * output_projection.size,
        read=2 * output_projection.size,
    )


def solution(mesh):
    placed = (
        P("groups", "wide"),
        P("wide"),
        P("groups"),
        P("groups"),
        P(None, "wide"),
        P("wide", None),
        P("wide", None),
        P(None, "wide"),
        P(("groups", "wide"), None, None),
        P(("groups", "wide"), None, None),
    )
    return jax.shard_map(
        functools.partial(body, mesh.shape["wide"]),
        mesh=mesh,
        in_specs=placed,
        out_specs=P("groups", "wide"),
        check_vma=False,
    )
```

```python
import functools
import math

import jax
import jax.numpy as jnp
import numpy as np
from jax import lax
from jax.experimental import pallas as pl
from jax.experimental.pallas import tpu as pltpu
from jax.sharding import PartitionSpec as P

QUERY_HEADS = 64
KEY_VALUE_HEADS = 4
HEAD_SIZE = 128
QUERY_GROUP = QUERY_HEADS // KEY_VALUE_HEADS

EPS = 1e-05
ROPE_BASE = 500000.0
MIB = 1 << 20
F32 = jnp.float32
BF16 = jnp.bfloat16


def call(kernel, out_shape, args, near=(), far=(), smem=(), scratch=(), limit=4 * MIB, flops=0, read=0):
    operands, specs = [], []
    for i, arg in enumerate(args):
        space = pltpu.SMEM if i in smem else pltpu.VMEM
        if i in near:
            arg = pltpu.with_memory_space_constraint(arg, pltpu.VMEM)
        if i in far:
            arg = pltpu.with_memory_space_constraint(arg, pltpu.HBM)
            space = pltpu.HBM
        operands.append(arg)
        specs.append(pl.BlockSpec(memory_space=space))
    return pl.pallas_call(
        kernel,
        out_shape=out_shape,
        in_specs=specs,
        out_specs=jax.tree.map(lambda _: pl.BlockSpec(memory_space=pltpu.VMEM), out_shape),
        scratch_shapes=list(scratch),
        compiler_params=pltpu.CompilerParams(vmem_limit_bytes=limit),
        cost_estimate=pl.CostEstimate(flops=flops, bytes_accessed=read, transcendentals=0),
    )(*operands)


def prepare_kernel(far_tokens, far_gain, far_slot, scaled_ref, squares_ref, tokens_ref, gain_ref, slot_ref, sems):
    copies = [
        pltpu.make_async_copy(far, near, sems.at[i])
        for i, (far, near) in enumerate(
            ((far_tokens, tokens_ref), (far_gain, gain_ref), (far_slot, slot_ref))
        )
    ]
    for copy in copies:
        copy.start()
    for copy in copies:
        copy.wait()
    rows, features = tokens_ref.shape
    wide_f = tokens_ref[...].astype(F32)
    squares = jnp.sum(wide_f * wide_f, axis=1, keepdims=True)
    gain = gain_ref[...].astype(F32).reshape(1, features)
    scaled = (wide_f * gain).astype(BF16)
    picked = lax.broadcasted_iota(jnp.int32, (rows, rows), 0) == slot_ref[...]
    scaled_ref[...] = jnp.dot(
        picked.astype(BF16), scaled, preferred_element_type=F32
    ).astype(BF16)
    turned = jnp.sum(jnp.where(picked, jnp.transpose(jnp.broadcast_to(squares, (rows, rows))), 0.0), axis=1, keepdims=True)
    squares_ref[...] = jnp.broadcast_to(turned, squares_ref.shape)


def join_kernel(mine_ref, arrived_ref, after_ref, joined_ref):
    count = mine_ref.shape[0]
    joined_ref[:count] = mine_ref[...]
    joined_ref[count:] = arrived_ref[...]


def share_kernel(scaled_ref, far_key, far_value, far_query, key_share_ref, value_share_ref, key_ref, value_ref, sems):
    copies = [
        pltpu.make_async_copy(far_key, key_ref, sems.at[0]),
        pltpu.make_async_copy(far_value, value_ref, sems.at[1]),
    ]
    for copy in copies:
        copy.start()
    copies[0].wait()
    key_share_ref[...] = jnp.dot(scaled_ref[...], key_ref[...], preferred_element_type=F32)
    copies[1].wait()
    value_share_ref[...] = jnp.dot(scaled_ref[...], value_ref[...], preferred_element_type=F32)


def products(offsets, first, blocks_ref, weight_ref, total):
    features = blocks_ref.shape[2]
    place = lax.axis_index("wide")
    for k, offset in enumerate(offsets):
        start = pl.multiple_of((place ^ offset) * features, features)
        total = total + jnp.dot(
            blocks_ref[first + k], weight_ref[pl.ds(start, features), :], preferred_element_type=F32
        )
    return total


def query_kernel(offsets, first, blocks_ref, weight_ref, total_ref, out_ref):
    out_ref[...] = products(offsets, first, blocks_ref, weight_ref, total_ref[...])


def query_turns_kernel(offsets, pairs, blocks_ref, weight_ref, lengths_ref, rate_ref, out_ref, turns_ref):
    out_ref[...] = products(offsets, 0, blocks_ref, weight_ref, jnp.zeros(out_ref.shape, F32))
    own = (lax.axis_index("wide") * pairs) % lengths_ref.shape[0]
    positions = jnp.concatenate(
        [jnp.full((1, HEAD_SIZE), lengths_ref[own + i], jnp.int32) for i in range(pairs)], 0
    )
    angle = positions.astype(F32) * rate_ref[...]
    turns_ref[0] = jnp.cos(angle)
    turns_ref[1] = jnp.sin(angle)


def message_kernel(
    offsets, pairs, blocks_ref, weight_ref, total_ref, key_ref, value_ref, squares_ref, message_ref
):
    query = products(offsets, 0, blocks_ref, weight_ref, total_ref[...])
    rows = query.shape[0]
    held = query.shape[1] // HEAD_SIZE
    for target in range(message_ref.shape[0]):
        head, first = target * pairs // rows, target * pairs % rows
        slots = slice(first, first + pairs)
        columns = slice(head * HEAD_SIZE, (head + 1) * HEAD_SIZE)
        sent = range(head, held, KEY_VALUE_HEADS) if held % KEY_VALUE_HEADS == 0 else range(held)
        at = 0
        for j in sent:
            message_ref[target, at : at + pairs, :] = query[slots, j * HEAD_SIZE : (j + 1) * HEAD_SIZE]
            at += pairs
        message_ref[target, at : at + pairs, :] = key_ref[slots, columns]
        message_ref[target, at + pairs : at + 2 * pairs, :] = value_ref[slots, columns]
        message_ref[target, at + 2 * pairs : at + 3 * pairs, :] = squares_ref[slots, :]


def rotated(values, cosines, sines):
    even = lax.broadcasted_iota(jnp.int32, values.shape, 1) % 2 == 0
    swapped = jnp.where(
        even, -pltpu.roll(values, HEAD_SIZE - 1, 1), pltpu.roll(values, 1, 1)
    )
    return values * cosines + swapped * sines


def side_by_side(ref, members, start, size):
    parts = [ref[i, start : start + size, :] for i in members]
    return parts[0] if len(parts) == 1 else jnp.concatenate(parts, axis=1)


def folded(op, array):
    tiles = [array[:, at : at + HEAD_SIZE] for at in range(0, array.shape[1], HEAD_SIZE)]
    while len(tiles) > 1:
        tiles = [op(*tiles[k : k + 2]) if k + 1 < len(tiles) else tiles[k] for k in range(0, len(tiles), 2)]
    return tiles[0]


def attend_kernel(
    pairs, width, lengths_ref, turns_ref, query_ref, rest_ref, keys_ref, values_ref, out_ref, scores_ref, wide_ref
):
    group = query_ref.shape[0]
    length = keys_ref.shape[1]
    first = (lax.axis_index("wide") * pairs) % lengths_ref.shape[0]
    at = rest_ref.shape[1] - 3 * pairs
    summed = jnp.sum(rest_ref[:, at:, :], axis=0)
    score_scale = 1.0 / math.sqrt(HEAD_SIZE)
    step = math.gcd(length, 512)
    many = 2 if pairs % 2 == 0 else 1
    parts = []
    for base in range(0, pairs, many):
        members = range(base, base + many)
        queries, owns, values, limits = [], [], [], []
        for i in members:
            scale = lax.rsqrt(summed[2 * pairs + i : 2 * pairs + i + 1, :] * (1.0 / width) + EPS)
            cosines, sines = turns_ref[0, i : i + 1, :], turns_ref[1, i : i + 1, :]
            query = rotated(query_ref[:, i, :] * scale, cosines, sines).astype(BF16)
            key = jnp.broadcast_to(summed[i : i + 1, :] * scale, (8, HEAD_SIZE))
            key = rotated(key, cosines, sines)[0:1, :].astype(BF16).astype(F32)
            values.append((summed[pairs + i : pairs + i + 1, :] * scale).astype(BF16).astype(F32))
            owns.append(jnp.sum(query.astype(F32) * key, axis=1, keepdims=True))
            limits.append(jnp.full((group, step), lengths_ref[first + i], jnp.int32))
            blank = jnp.zeros_like(query)
            queries.append(
                query
                if many == 1
                else jnp.concatenate([query if j == i else blank for j in members], axis=1)
            )
        stacked = jnp.concatenate(queries, axis=0)
        own = jnp.concatenate(owns, axis=0)
        limit = jnp.concatenate(limits, axis=0)
        column = lax.broadcasted_iota(jnp.int32, (many * group, step), 1)
        tops = jnp.broadcast_to(own, (many * group, HEAD_SIZE))
        place = base // many
        for start in range(0, length, step):
            scores = lax.dot_general(
                stacked,
                side_by_side(keys_ref, members, start, step),
                (((1,), (1,)), ((), ())),
                preferred_element_type=F32,
            )
            scores = jnp.where(column < limit - start, scores, -jnp.inf)
            scores_ref[place, :, start : start + step] = scores
            tops = jnp.maximum(tops, folded(jnp.maximum, scores))
        parts.append((members, place, own, tops, values))
    factor = score_scale * math.log2(math.e)
    weighed = []
    for members, place, own, tops, values in parts:
        top = jnp.max(tops, axis=1, keepdims=True)
        own_w = jnp.exp2((own - top) * factor)
        sums = jnp.zeros_like(tops)
        for start in range(0, length, step):
            weights = jnp.exp2((scores_ref[place, :, start : start + step] - top) * factor)
            scores_ref[place, :, start : start + step] = weights
            sums = sums + folded(jnp.add, weights)
        share = 1.0 / (own_w + jnp.sum(sums, axis=1, keepdims=True))
        weighed.append((members, place, share, (own_w * share).astype(BF16).astype(F32), values))
    for members, place, share, own_p, values in weighed:
        blended = jnp.zeros((many * group, many * HEAD_SIZE), F32)
        for start in range(0, length, step):
            blended = blended + jnp.dot(
                (scores_ref[place, :, start : start + step] * share).astype(BF16),
                side_by_side(values_ref, members, start, step),
                preferred_element_type=F32,
            )
        for k, i in enumerate(members):
            rows = slice(k * group, (k + 1) * group)
            result = blended[rows, k * HEAD_SIZE : (k + 1) * HEAD_SIZE] + own_p[rows] * values[k]
            for g in range(group):
                wide_ref[i : i + 1, g * HEAD_SIZE : (g + 1) * HEAD_SIZE] = result[g : g + 1, :]
    out_ref[...] = wide_ref[...].astype(BF16)


def place_rows(pairs, head_offsets, slot_offsets, slot_ref, pieces, left_ref, before_ref=None):
    rows = left_ref.shape[0]
    heads, held, _ = pieces[0].shape
    devices_of_head = rows // pairs
    place = lax.axis_index("wide")
    group_place = place % devices_of_head
    head_place = place // devices_of_head
    slot_of_row = jnp.transpose(jnp.broadcast_to(slot_ref[...], (rows, rows)))[:, 0:1]
    position = lax.broadcasted_iota(jnp.int32, (rows, held), 1)
    picks = []
    for offsets in slot_offsets:
        device = jnp.zeros_like(position)
        for k, offset in enumerate(offsets):
            device = jnp.where(position // pairs == k, group_place ^ offset, device)
        picks.append((slot_of_row == device * pairs + position % pairs).astype(BF16))
    for z, offset in enumerate(head_offsets):
        head = head_place ^ offset
        ordered = sum(
            jnp.dot(pick, piece[z], preferred_element_type=F32) for pick, piece in zip(picks, pieces)
        ).astype(BF16)
        for g in range(QUERY_GROUP):
            start = pl.multiple_of((g * heads + head) * HEAD_SIZE, HEAD_SIZE)
            columns = ordered[:, g * HEAD_SIZE : (g + 1) * HEAD_SIZE]
            if before_ref is not None:
                columns = columns + before_ref[:, pl.ds(start, HEAD_SIZE)]
            left_ref[:, pl.ds(start, HEAD_SIZE)] = columns


def assemble_kernel(pairs, head_offsets, slot_offsets, slot_ref, *refs):
    place_rows(pairs, head_offsets, slot_offsets, slot_ref, refs[:-1], refs[-1])


def project_kernel(
    pairs, head_offsets, slot_offsets, slot_ref, piece_ref, before_ref, weight_ref, out_ref, left_ref
):
    place_rows(pairs, head_offsets, slot_offsets, slot_ref, (piece_ref,), left_ref, before_ref)
    out_ref[...] = jnp.dot(
        left_ref[...], weight_ref[...], preferred_element_type=F32
    ).astype(BF16)


def swap(array, bit, count):
    return lax.ppermute(array, "wide", [(i, i ^ bit) for i in range(count)])


def body(
    count,
    tokens,
    norm_gain,
    slot_of_row,
    lengths,
    w_query,
    key_projection,
    value_projection,
    output_projection,
    slot_key_cache,
    slot_value_cache,
):
    rows, features = tokens.shape
    pairs = slot_key_cache.shape[0]
    width = w_query.shape[0]
    query_columns = w_query.shape[1]
    held = query_columns // HEAD_SIZE
    devices_of_head = rows // pairs
    bits = [1 << b for b in reversed(range(count.bit_length() - 1))]

    scaled, squares = call(
        prepare_kernel,
        (
            jax.ShapeDtypeStruct((rows, features), BF16),
            jax.ShapeDtypeStruct((rows, HEAD_SIZE), F32),
        ),
        (tokens, norm_gain, slot_of_row.reshape(1, rows)),
        far=(0, 1, 2),
        scratch=(
            pltpu.VMEM((rows, features), BF16),
            pltpu.VMEM((features,), BF16),
            pltpu.VMEM((1, rows), jnp.int32),
            pltpu.SemaphoreType.DMA((3,)),
        ),
    )

    index = np.arange(HEAD_SIZE)
    rate = (ROPE_BASE ** (-(index - index % 2) / HEAD_SIZE)).astype(np.float32)[None, :]
    totals = jax.ShapeDtypeStruct((rows, query_columns), F32)
    shares = jax.ShapeDtypeStruct((rows, key_projection.shape[1]), F32)

    def query(offsets, first, array, total):
        return call(
            functools.partial(query_kernel, tuple(offsets), first),
            totals,
            (array, w_query, total),
            near=(0, 1),
            flops=2 * rows * len(offsets) * features * query_columns,
            read=2 * len(offsets) * features * query_columns,
        )

    *outer, bit, core = bits
    blocks, offsets, new, total = scaled[None], [0], [0], None
    for far in (*outer, bit):
        arrived = swap(blocks, far, count)
        if len(offsets) == 1:
            after = key_share, value_share = call(
                share_kernel,
                (shares, shares),
                (scaled, key_projection, value_projection, w_query),
                near=(0,),
                far=(1, 2, 3),
                scratch=(
                    pltpu.VMEM(key_projection.shape, BF16),
                    pltpu.VMEM(value_projection.shape, BF16),
                    pltpu.SemaphoreType.DMA((2,)),
                ),
                flops=4 * rows * key_projection.size,
                read=8 * w_query.size,
            )
        elif total is None:
            after = total, turns = call(
                functools.partial(query_turns_kernel, tuple(offsets), pairs),
                (totals, jax.ShapeDtypeStruct((2, pairs, HEAD_SIZE), F32)),
                (blocks, w_query, lengths, jnp.asarray(rate)),
                near=(0, 1),
                smem=(2,),
                flops=2 * rows * len(offsets) * features * query_columns,
                read=2 * len(offsets) * features * query_columns,
            )
        else:
            total = query(new, len(offsets) - len(new), blocks, total)
            after = (total,)
        blocks = call(
            join_kernel,
            jax.ShapeDtypeStruct((2 * len(offsets), rows, features), BF16),
            (blocks, arrived, after[0]),
        )
        new = [o ^ far for o in offsets]
        offsets = offsets + new
    arrived = swap(blocks, core, count)
    total = query(new, len(offsets) - len(new), blocks, total)
    sent = held // KEY_VALUE_HEADS if held % KEY_VALUE_HEADS == 0 else held
    message = call(
        functools.partial(message_kernel, tuple(o ^ core for o in offsets), pairs),
        jax.ShapeDtypeStruct((count, pairs * (sent + 3), HEAD_SIZE), F32),
        (arrived, w_query, total, key_share, value_share, squares),
        near=(0, 1),
        flops=2 * arrived.size * query_columns,
        read=2 * len(offsets) * features * query_columns,
    )

    got = lax.all_to_all(message, "wide", 0, 0, tiled=True)
    if sent == 1 and held % KEY_VALUE_HEADS == 0:
        query_rows = got
    else:
        query_rows = (
            got[:, : pairs * sent].reshape(count, sent, pairs, HEAD_SIZE).reshape(-1, pairs, HEAD_SIZE)
        )
        if held % KEY_VALUE_HEADS:
            head = lax.axis_index("wide") // devices_of_head
            query_rows = lax.dynamic_index_in_dim(
                query_rows.reshape(QUERY_GROUP, KEY_VALUE_HEADS, pairs, HEAD_SIZE), head, 1, False
            )
    cache_bytes = 2 * slot_key_cache.size
    attended = call(
        functools.partial(attend_kernel, pairs, width),
        jax.ShapeDtypeStruct((pairs, QUERY_GROUP * HEAD_SIZE), BF16),
        (lengths, turns, query_rows, got, slot_key_cache, slot_value_cache),
        near=(4, 5),
        smem=(0,),
        scratch=(
            pltpu.VMEM(
                ((pairs + 1) // 2, min(pairs, 2) * QUERY_GROUP, slot_key_cache.shape[1]), F32
            ),
            pltpu.VMEM((pairs, QUERY_GROUP * HEAD_SIZE), F32),
        ),
        limit=8 * MIB,
        flops=4 * QUERY_GROUP * slot_key_cache.size,
        read=2 * cache_bytes,
    )

    mine = attended[None]
    head_offsets, slot_offsets = [0], [0]
    for far in outer:
        arrived = swap(mine, far, count)
        if far >= devices_of_head:
            mine = jnp.concatenate([mine, arrived], 0)
            head_offsets = head_offsets + [o ^ (far // devices_of_head) for o in head_offsets]
        else:
            mine = jnp.concatenate([mine, arrived], 1)
            slot_offsets = slot_offsets + [o ^ far for o in slot_offsets]
    across = swap(mine, bit, count)
    beside = swap(mine, core, count)
    both = swap(across, core, count)
    slot_row = slot_of_row.reshape(1, rows)
    left = jax.ShapeDtypeStruct((rows, output_projection.shape[0]), BF16)
    before = call(
        functools.partial(
            assemble_kernel,
            pairs,
            tuple(head_offsets),
            tuple(tuple(o ^ b for o in slot_offsets) for b in (0, core, bit)),
        ),
        left,
        (slot_row, mine, beside, across),
    )
    return call(
        functools.partial(
            project_kernel,
            pairs,
            tuple(head_offsets),
            (tuple(o ^ bit ^ core for o in slot_offsets),),
        ),
        jax.ShapeDtypeStruct((rows, output_projection.shape[1]), BF16),
        (slot_row, both, before, output_projection),
        near=(3,),
        scratch=(pltpu.VMEM(left.shape, BF16),),
        flops=2 * rows * output_projection.size,
        read=2 * output_projection.size,
    )


def solution(mesh):
    placed = (
        P("groups", "wide"),
        P("wide"),
        P("groups"),
        P("groups"),
        P(None, "wide"),
        P("wide", None),
        P("wide", None),
        P(None, "wide"),
        P(("groups", "wide"), None, None),
        P(("groups", "wide"), None, None),
    )
    return jax.shard_map(
        functools.partial(body, mesh.shape["wide"]),
        mesh=mesh,
        in_specs=placed,
        out_specs=P("groups", "wide"),
        check_vma=False,
    )
```

```python
import functools
import math

import jax
import jax.numpy as jnp
import numpy as np
from jax import lax
from jax.experimental import pallas as pl
from jax.experimental.pallas import tpu as pltpu
from jax.sharding import PartitionSpec as P

QUERY_HEADS = 64
KEY_VALUE_HEADS = 4
HEAD_SIZE = 128
QUERY_GROUP = QUERY_HEADS // KEY_VALUE_HEADS

EPS = 1e-05
ROPE_BASE = 500000.0
MIB = 1 << 20
F32 = jnp.float32
BF16 = jnp.bfloat16


def call(kernel, out_shape, args, near=(), far=(), smem=(), scratch=(), limit=4 * MIB, flops=0, read=0):
    operands, specs = [], []
    for i, arg in enumerate(args):
        space = pltpu.SMEM if i in smem else pltpu.VMEM
        if i in near:
            arg = pltpu.with_memory_space_constraint(arg, pltpu.VMEM)
        if i in far:
            arg = pltpu.with_memory_space_constraint(arg, pltpu.HBM)
            space = pltpu.HBM
        operands.append(arg)
        specs.append(pl.BlockSpec(memory_space=space))
    return pl.pallas_call(
        kernel,
        out_shape=out_shape,
        in_specs=specs,
        out_specs=jax.tree.map(lambda _: pl.BlockSpec(memory_space=pltpu.VMEM), out_shape),
        scratch_shapes=list(scratch),
        compiler_params=pltpu.CompilerParams(vmem_limit_bytes=limit),
        cost_estimate=pl.CostEstimate(flops=flops, bytes_accessed=read, transcendentals=0),
    )(*operands)


def prepare_kernel(far_tokens, far_gain, far_slot, scaled_ref, squares_ref, tokens_ref, gain_ref, slot_ref, sems):
    copies = [
        pltpu.make_async_copy(far, near, sems.at[i])
        for i, (far, near) in enumerate(
            ((far_tokens, tokens_ref), (far_gain, gain_ref), (far_slot, slot_ref))
        )
    ]
    for copy in copies:
        copy.start()
    for copy in copies:
        copy.wait()
    rows, features = tokens_ref.shape
    wide_f = tokens_ref[...].astype(F32)
    squares = jnp.sum(wide_f * wide_f, axis=1, keepdims=True)
    gain = gain_ref[...].astype(F32).reshape(1, features)
    scaled = (wide_f * gain).astype(BF16)
    picked = lax.broadcasted_iota(jnp.int32, (rows, rows), 0) == slot_ref[...]
    scaled_ref[...] = jnp.dot(
        picked.astype(BF16), scaled, preferred_element_type=F32
    ).astype(BF16)
    turned = jnp.sum(jnp.where(picked, jnp.transpose(jnp.broadcast_to(squares, (rows, rows))), 0.0), axis=1, keepdims=True)
    squares_ref[...] = jnp.broadcast_to(turned, squares_ref.shape)


def pass_kernel(array_ref, after_ref, same_ref):
    same_ref[...] = array_ref[...]


def join_kernel(mine_ref, arrived_ref, after_ref, joined_ref):
    count = mine_ref.shape[0]
    joined_ref[:count] = mine_ref[...]
    joined_ref[count:] = arrived_ref[...]


def share_kernel(scaled_ref, far_key, far_value, far_query, key_share_ref, value_share_ref, key_ref, value_ref, sems):
    copies = [
        pltpu.make_async_copy(far_key, key_ref, sems.at[0]),
        pltpu.make_async_copy(far_value, value_ref, sems.at[1]),
    ]
    for copy in copies:
        copy.start()
    copies[0].wait()
    key_share_ref[...] = jnp.dot(scaled_ref[...], key_ref[...], preferred_element_type=F32)
    copies[1].wait()
    value_share_ref[...] = jnp.dot(scaled_ref[...], value_ref[...], preferred_element_type=F32)


def products(offsets, first, blocks_ref, weight_ref, total):
    features = blocks_ref.shape[2]
    place = lax.axis_index("wide")
    for k, offset in enumerate(offsets):
        start = pl.multiple_of((place ^ offset) * features, features)
        total = total + jnp.dot(
            blocks_ref[first + k], weight_ref[pl.ds(start, features), :], preferred_element_type=F32
        )
    return total


def query_kernel(offsets, first, blocks_ref, weight_ref, total_ref, out_ref):
    out_ref[...] = products(offsets, first, blocks_ref, weight_ref, total_ref[...])


def query_turns_kernel(offsets, pairs, blocks_ref, weight_ref, lengths_ref, rate_ref, out_ref, turns_ref, limits_ref):
    out_ref[...] = products(offsets, 0, blocks_ref, weight_ref, jnp.zeros(out_ref.shape, F32))
    own = (lax.axis_index("wide") * pairs) % lengths_ref.shape[0]
    positions = jnp.concatenate(
        [jnp.full((1, HEAD_SIZE), lengths_ref[own + i], jnp.int32) for i in range(pairs)], 0
    )
    angle = positions.astype(F32) * rate_ref[...]
    turns_ref[0] = jnp.cos(angle)
    turns_ref[1] = jnp.sin(angle)
    limits_ref[...] = positions


def message_kernel(
    offsets, pairs, blocks_ref, weight_ref, total_ref, key_ref, value_ref, squares_ref, message_ref
):
    query = products(offsets, 0, blocks_ref, weight_ref, total_ref[...])
    rows = query.shape[0]
    held = query.shape[1] // HEAD_SIZE
    for target in range(message_ref.shape[0]):
        head, first = target * pairs // rows, target * pairs % rows
        slots = slice(first, first + pairs)
        columns = slice(head * HEAD_SIZE, (head + 1) * HEAD_SIZE)
        sent = range(head, held, KEY_VALUE_HEADS) if held % KEY_VALUE_HEADS == 0 else range(held)
        at = 0
        for j in sent:
            message_ref[target, at : at + pairs, :] = query[slots, j * HEAD_SIZE : (j + 1) * HEAD_SIZE]
            at += pairs
        message_ref[target, at : at + pairs, :] = key_ref[slots, columns]
        message_ref[target, at + pairs : at + 2 * pairs, :] = value_ref[slots, columns]
        message_ref[target, at + 2 * pairs : at + 3 * pairs, :] = squares_ref[slots, :]


def rotated(values, cosines, sines):
    even = lax.broadcasted_iota(jnp.int32, values.shape, 1) % 2 == 0
    swapped = jnp.where(
        even, -pltpu.roll(values, HEAD_SIZE - 1, 1), pltpu.roll(values, 1, 1)
    )
    return values * cosines + swapped * sines


def side_by_side(ref, members, start, size):
    parts = [ref[i, start : start + size, :] for i in members]
    return parts[0] if len(parts) == 1 else jnp.concatenate(parts, axis=1)


def folded(op, array):
    tiles = [array[:, at : at + HEAD_SIZE] for at in range(0, array.shape[1], HEAD_SIZE)]
    while len(tiles) > 1:
        tiles = [op(*tiles[k : k + 2]) if k + 1 < len(tiles) else tiles[k] for k in range(0, len(tiles), 2)]
    return tiles[0]


def attend_kernel(
    pairs, width, limits_ref, turns_ref, query_ref, rest_ref, keys_ref, values_ref, out_ref, scores_ref, wide_ref
):
    group = query_ref.shape[0]
    length = keys_ref.shape[1]
    at = rest_ref.shape[1] - 3 * pairs
    summed = jnp.sum(rest_ref[:, at:, :], axis=0)
    score_scale = 1.0 / math.sqrt(HEAD_SIZE)
    step = math.gcd(length, 512)
    many = 2 if pairs % 2 == 0 else 1
    parts = []
    for base in range(0, pairs, many):
        members = range(base, base + many)
        queries, owns, values, limits = [], [], [], []
        for i in members:
            scale = lax.rsqrt(summed[2 * pairs + i : 2 * pairs + i + 1, :] * (1.0 / width) + EPS)
            cosines, sines = turns_ref[0, i : i + 1, :], turns_ref[1, i : i + 1, :]
            query = rotated(query_ref[:, i, :] * scale, cosines, sines).astype(BF16)
            key = jnp.broadcast_to(summed[i : i + 1, :] * scale, (8, HEAD_SIZE))
            key = rotated(key, cosines, sines)[0:1, :].astype(BF16).astype(F32)
            values.append((summed[pairs + i : pairs + i + 1, :] * scale).astype(BF16).astype(F32))
            owns.append(jnp.sum(query.astype(F32) * key, axis=1, keepdims=True))
            limits.append(jnp.broadcast_to(limits_ref[i : i + 1, :], (group, HEAD_SIZE)))
            blank = jnp.zeros_like(query)
            queries.append(
                query
                if many == 1
                else jnp.concatenate([query if j == i else blank for j in members], axis=1)
            )
        stacked = jnp.concatenate(queries, axis=0)
        own = jnp.concatenate(owns, axis=0)
        limit = jnp.concatenate(limits, axis=0)
        column = lax.broadcasted_iota(jnp.int32, (many * group, HEAD_SIZE), 1)
        tops = jnp.broadcast_to(own, (many * group, HEAD_SIZE))
        place = base // many
        for start in range(0, length, step):
            scores = lax.dot_general(
                stacked,
                side_by_side(keys_ref, members, start, step),
                (((1,), (1,)), ((), ())),
                preferred_element_type=F32,
            )
            for at in range(0, step, HEAD_SIZE):
                tile = jnp.where(
                    column < limit - (start + at), scores[:, at : at + HEAD_SIZE], -jnp.inf
                )
                scores_ref[place, :, start + at : start + at + HEAD_SIZE] = tile
                tops = jnp.maximum(tops, tile)
        parts.append((members, place, own, tops, values))
    factor = score_scale * math.log2(math.e)
    for members, place, own, tops, values in parts:
        top = jnp.max(tops, axis=1, keepdims=True)
        own_w = jnp.exp2((own - top) * factor)
        sums = jnp.zeros_like(tops)
        blended = jnp.zeros((many * group, many * HEAD_SIZE), F32)
        for start in range(0, length, step):
            weights = jnp.exp2((scores_ref[place, :, start : start + step] - top) * factor)
            sums = sums + folded(jnp.add, weights)
            blended = blended + jnp.dot(
                weights.astype(BF16),
                side_by_side(values_ref, members, start, step),
                preferred_element_type=F32,
            )
        share = 1.0 / (own_w + jnp.sum(sums, axis=1, keepdims=True))
        blended = blended * share
        own_p = (own_w * share).astype(BF16).astype(F32)
        for k, i in enumerate(members):
            rows = slice(k * group, (k + 1) * group)
            result = blended[rows, k * HEAD_SIZE : (k + 1) * HEAD_SIZE] + own_p[rows] * values[k]
            for g in range(group):
                wide_ref[i : i + 1, g * HEAD_SIZE : (g + 1) * HEAD_SIZE] = result[g : g + 1, :]
    out_ref[...] = wide_ref[...].astype(BF16)


def project_half(pairs, head_offsets, slot_offsets, slot_ref, pieces, weight_ref, total):
    rows = slot_ref.shape[1]
    held = pieces[0].shape[1]
    devices_of_head = rows // pairs
    place = lax.axis_index("wide")
    group_place = place % devices_of_head
    head_place = place // devices_of_head
    slot_of_row = jnp.transpose(jnp.broadcast_to(slot_ref[...], (rows, rows)))[:, 0:1]
    position = lax.broadcasted_iota(jnp.int32, (rows, held), 1)
    picks = []
    for offsets in slot_offsets:
        device = jnp.zeros_like(position)
        for k, offset in enumerate(offsets):
            device = jnp.where(position // pairs == k, group_place ^ offset, device)
        picks.append((slot_of_row == device * pairs + position % pairs).astype(BF16))
    ordered = [
        sum(
            jnp.dot(pick, piece[z], preferred_element_type=F32) for pick, piece in zip(picks, pieces)
        ).astype(BF16)
        for z in range(len(head_offsets))
    ]
    for g in range(QUERY_GROUP):
        columns = slice(g * HEAD_SIZE, (g + 1) * HEAD_SIZE)
        weights = []
        for offset in head_offsets:
            start = (g * KEY_VALUE_HEADS + (head_place ^ offset)) * HEAD_SIZE
            weights.append(weight_ref[pl.ds(pl.multiple_of(start, HEAD_SIZE), HEAD_SIZE), :])
        total = total + jnp.dot(
            jnp.concatenate([o[:, columns] for o in ordered], axis=1),
            jnp.concatenate(weights, axis=0),
            preferred_element_type=F32,
        )
    return total


def first_half_kernel(pairs, head_offsets, slot_offsets, slot_ref, mine_ref, other_ref, weight_ref, out_ref):
    out_ref[...] = project_half(
        pairs,
        head_offsets,
        slot_offsets,
        slot_ref,
        (mine_ref, other_ref),
        weight_ref,
        jnp.zeros(out_ref.shape, F32),
    )


def second_half_kernel(
    pairs, head_offsets, slot_offsets, slot_ref, mine_ref, other_ref, weight_ref, half_ref, out_ref
):
    out_ref[...] = project_half(
        pairs, head_offsets, slot_offsets, slot_ref, (mine_ref, other_ref), weight_ref, half_ref[...]
    ).astype(BF16)


def swap(array, bit, count):
    return lax.ppermute(array, "wide", [(i, i ^ bit) for i in range(count)])


def body(
    count,
    tokens,
    norm_gain,
    slot_of_row,
    lengths,
    w_query,
    key_projection,
    value_projection,
    output_projection,
    slot_key_cache,
    slot_value_cache,
):
    rows, features = tokens.shape
    pairs = slot_key_cache.shape[0]
    width = w_query.shape[0]
    query_columns = w_query.shape[1]
    held = query_columns // HEAD_SIZE
    devices_of_head = rows // pairs
    bits = [1 << b for b in reversed(range(count.bit_length() - 1))]

    scaled, squares = call(
        prepare_kernel,
        (
            jax.ShapeDtypeStruct((rows, features), BF16),
            jax.ShapeDtypeStruct((rows, HEAD_SIZE), F32),
        ),
        (tokens, norm_gain, slot_of_row.reshape(1, rows)),
        far=(0, 1, 2),
        scratch=(
            pltpu.VMEM((rows, features), BF16),
            pltpu.VMEM((features,), BF16),
            pltpu.VMEM((1, rows), jnp.int32),
            pltpu.SemaphoreType.DMA((3,)),
        ),
    )

    index = np.arange(HEAD_SIZE)
    rate = (ROPE_BASE ** (-(index - index % 2) / HEAD_SIZE)).astype(np.float32)[None, :]
    totals = jax.ShapeDtypeStruct((rows, query_columns), F32)
    shares = jax.ShapeDtypeStruct((rows, key_projection.shape[1]), F32)

    def query(offsets, first, array, total):
        return call(
            functools.partial(query_kernel, tuple(offsets), first),
            totals,
            (array, w_query, total),
            near=(0, 1),
            flops=2 * rows * len(offsets) * features * query_columns,
            read=2 * len(offsets) * features * query_columns,
        )

    *outer, bit, core = bits
    blocks, offsets, new, total = scaled[None], [0], [0], None
    for far in (*outer, bit):
        arrived = swap(blocks, far, count)
        if len(offsets) == 1:
            after = key_share, value_share = call(
                share_kernel,
                (shares, shares),
                (scaled, key_projection, value_projection, w_query),
                near=(0,),
                far=(1, 2, 3),
                scratch=(
                    pltpu.VMEM(key_projection.shape, BF16),
                    pltpu.VMEM(value_projection.shape, BF16),
                    pltpu.SemaphoreType.DMA((2,)),
                ),
                flops=4 * rows * key_projection.size,
                read=8 * w_query.size,
            )
        elif total is None:
            after = total, turns, limits = call(
                functools.partial(query_turns_kernel, tuple(offsets), pairs),
                (
                    totals,
                    jax.ShapeDtypeStruct((2, pairs, HEAD_SIZE), F32),
                    jax.ShapeDtypeStruct((pairs, HEAD_SIZE), jnp.int32),
                ),
                (blocks, w_query, lengths, jnp.asarray(rate)),
                near=(0, 1),
                smem=(2,),
                flops=2 * rows * len(offsets) * features * query_columns,
                read=2 * len(offsets) * features * query_columns,
            )
        else:
            total = query(new, len(offsets) - len(new), blocks, total)
            after = (total,)
        blocks = call(
            join_kernel,
            jax.ShapeDtypeStruct((2 * len(offsets), rows, features), BF16),
            (blocks, arrived, after[0]),
        )
        new = [o ^ far for o in offsets]
        offsets = offsets + new
    arrived = swap(blocks, core, count)
    total = query(new, len(offsets) - len(new), blocks, total)
    sent = held // KEY_VALUE_HEADS if held % KEY_VALUE_HEADS == 0 else held
    message = call(
        functools.partial(message_kernel, tuple(o ^ core for o in offsets), pairs),
        jax.ShapeDtypeStruct((count, pairs * (sent + 3), HEAD_SIZE), F32),
        (arrived, w_query, total, key_share, value_share, squares),
        near=(0, 1),
        flops=2 * arrived.size * query_columns,
        read=2 * len(offsets) * features * query_columns,
    )

    got = lax.all_to_all(message, "wide", 0, 0, tiled=True)
    if sent == 1 and held % KEY_VALUE_HEADS == 0:
        query_rows = got
    else:
        query_rows = (
            got[:, : pairs * sent].reshape(count, sent, pairs, HEAD_SIZE).reshape(-1, pairs, HEAD_SIZE)
        )
        if held % KEY_VALUE_HEADS:
            head = lax.axis_index("wide") // devices_of_head
            query_rows = lax.dynamic_index_in_dim(
                query_rows.reshape(QUERY_GROUP, KEY_VALUE_HEADS, pairs, HEAD_SIZE), head, 1, False
            )
    cache_bytes = 2 * slot_key_cache.size
    attended = call(
        functools.partial(attend_kernel, pairs, width),
        jax.ShapeDtypeStruct((pairs, QUERY_GROUP * HEAD_SIZE), BF16),
        (limits, turns, query_rows, got, slot_key_cache, slot_value_cache),
        near=(4, 5),
        scratch=(
            pltpu.VMEM(
                ((pairs + 1) // 2, min(pairs, 2) * QUERY_GROUP, slot_key_cache.shape[1]), F32
            ),
            pltpu.VMEM((pairs, QUERY_GROUP * HEAD_SIZE), F32),
        ),
        limit=8 * MIB,
        flops=4 * QUERY_GROUP * slot_key_cache.size,
        read=2 * cache_bytes,
    )

    mine = attended[None]
    slot_offsets = [0]
    for far in bits:
        if core < far < devices_of_head:
            mine = jnp.concatenate([mine, swap(mine, far, count)], 1)
            slot_offsets = slot_offsets + [o ^ far for o in slot_offsets]
    high, low = bits[0] // devices_of_head, bits[1] // devices_of_head
    mine = jnp.concatenate([mine, swap(mine, bits[0], count)], 0)
    across = swap(mine, bits[1], count)
    beside = swap(mine, core, count)
    slots = (tuple(slot_offsets), tuple(o ^ core for o in slot_offsets))
    slot_row = slot_of_row.reshape(1, rows)
    columns = output_projection.shape[1]
    half = call(
        functools.partial(first_half_kernel, pairs, (0, high), slots),
        jax.ShapeDtypeStruct((rows, columns), F32),
        (slot_row, mine, beside, output_projection),
        near=(3,),
        flops=rows * output_projection.size,
        read=output_projection.size,
    )
    across = call(pass_kernel, jax.ShapeDtypeStruct(across.shape, BF16), (across, half))
    both = swap(across, core, count)
    return call(
        functools.partial(second_half_kernel, pairs, (low, low ^ high), slots),
        jax.ShapeDtypeStruct((rows, columns), BF16),
        (slot_row, across, both, output_projection, half),
        near=(3,),
        flops=rows * output_projection.size,
        read=output_projection.size,
    )


def solution(mesh):
    placed = (
        P("groups", "wide"),
        P("wide"),
        P("groups"),
        P("groups"),
        P(None, "wide"),
        P("wide", None),
        P("wide", None),
        P(None, "wide"),
        P(("groups", "wide"), None, None),
        P(("groups", "wide"), None, None),
    )
    return jax.shard_map(
        functools.partial(body, mesh.shape["wide"]),
        mesh=mesh,
        in_specs=placed,
        out_specs=P("groups", "wide"),
        check_vma=False,
    )
```

```python
import functools
import math

import jax
import jax.numpy as jnp
import numpy as np
from jax import lax
from jax.experimental import pallas as pl
from jax.experimental.pallas import tpu as pltpu
from jax.sharding import PartitionSpec as P

QUERY_HEADS = 64
KEY_VALUE_HEADS = 4
HEAD_SIZE = 128
QUERY_GROUP = QUERY_HEADS // KEY_VALUE_HEADS

EPS = 1e-05
ROPE_BASE = 500000.0
MIB = 1 << 20
F32 = jnp.float32
BF16 = jnp.bfloat16


def call(kernel, out_shape, args, near=(), far=(), smem=(), scratch=(), limit=4 * MIB, flops=0, read=0):
    operands, specs = [], []
    for i, arg in enumerate(args):
        space = pltpu.SMEM if i in smem else pltpu.VMEM
        if i in near:
            arg = pltpu.with_memory_space_constraint(arg, pltpu.VMEM)
        if i in far:
            arg = pltpu.with_memory_space_constraint(arg, pltpu.HBM)
            space = pltpu.HBM
        operands.append(arg)
        specs.append(pl.BlockSpec(memory_space=space))
    return pl.pallas_call(
        kernel,
        out_shape=out_shape,
        in_specs=specs,
        out_specs=jax.tree.map(lambda _: pl.BlockSpec(memory_space=pltpu.VMEM), out_shape),
        scratch_shapes=list(scratch),
        compiler_params=pltpu.CompilerParams(vmem_limit_bytes=limit),
        cost_estimate=pl.CostEstimate(flops=flops, bytes_accessed=read, transcendentals=0),
    )(*operands)


def fetch(pairs, sems):
    copies = [pltpu.make_async_copy(far, near, sems.at[i]) for i, (far, near) in enumerate(pairs)]
    for copy in copies:
        copy.start()
    return copies


def picked_rows(slot_ref):
    rows = slot_ref.shape[1]
    return lax.broadcasted_iota(jnp.int32, (rows, rows), 0) == slot_ref[...]


def prepare_kernel(
    far_tokens, far_gain, far_slot, far_query, scaled_ref, tokens_ref, gain_ref, slot_ref, sems
):
    for copy in fetch(((far_tokens, tokens_ref), (far_gain, gain_ref), (far_slot, slot_ref)), sems):
        copy.wait()
    gain = gain_ref[...].astype(F32).reshape(1, gain_ref.shape[0])
    scaled = (tokens_ref[...].astype(F32) * gain).astype(BF16)
    scaled_ref[...] = jnp.dot(
        picked_rows(slot_ref).astype(BF16), scaled, preferred_element_type=F32
    ).astype(BF16)


def pass_kernel(array_ref, *refs):
    refs[-1][...] = array_ref[...]


def join_kernel(mine_ref, arrived_ref, *refs):
    joined_ref = refs[-1]
    count = mine_ref.shape[0]
    joined_ref[:count] = mine_ref[...]
    joined_ref[count:] = arrived_ref[...]


def share_kernel(
    scaled_ref,
    far_tokens,
    far_slot,
    far_key,
    far_value,
    after_ref,
    key_share_ref,
    value_share_ref,
    squares_ref,
    tokens_ref,
    slot_ref,
    key_ref,
    value_ref,
    sems,
):
    copies = fetch(
        ((far_tokens, tokens_ref), (far_slot, slot_ref), (far_key, key_ref), (far_value, value_ref)), sems
    )
    copies[0].wait()
    copies[1].wait()
    rows = tokens_ref.shape[0]
    wide_f = tokens_ref[...].astype(F32)
    squares = jnp.sum(wide_f * wide_f, axis=1, keepdims=True)
    turned = jnp.transpose(jnp.broadcast_to(squares, (rows, rows)))
    squares = jnp.sum(jnp.where(picked_rows(slot_ref), turned, 0.0), axis=1, keepdims=True)
    squares_ref[...] = jnp.broadcast_to(squares, squares_ref.shape)
    copies[2].wait()
    key_share_ref[...] = jnp.dot(scaled_ref[...], key_ref[...], preferred_element_type=F32)
    copies[3].wait()
    value_share_ref[...] = jnp.dot(scaled_ref[...], value_ref[...], preferred_element_type=F32)


def products(offsets, first, blocks_ref, weight_ref, total):
    features = blocks_ref.shape[2]
    place = lax.axis_index("wide")
    for k, offset in enumerate(offsets):
        start = pl.multiple_of((place ^ offset) * features, features)
        total = total + jnp.dot(
            blocks_ref[first + k], weight_ref[pl.ds(start, features), :], preferred_element_type=F32
        )
    return total


def query_kernel(offsets, first, blocks_ref, weight_ref, total_ref, out_ref):
    out_ref[...] = products(offsets, first, blocks_ref, weight_ref, total_ref[...])


def query_turns_kernel(offsets, pairs, blocks_ref, weight_ref, lengths_ref, rate_ref, out_ref, turns_ref, limits_ref):
    out_ref[...] = products(offsets, 0, blocks_ref, weight_ref, jnp.zeros(out_ref.shape, F32))
    own = (lax.axis_index("wide") * pairs) % lengths_ref.shape[0]
    positions = jnp.concatenate(
        [jnp.full((1, HEAD_SIZE), lengths_ref[own + i], jnp.int32) for i in range(pairs)], 0
    )
    angle = positions.astype(F32) * rate_ref[...]
    turns_ref[0] = jnp.cos(angle)
    turns_ref[1] = jnp.sin(angle)
    limits_ref[...] = positions


def message_kernel(
    offsets, pairs, blocks_ref, weight_ref, total_ref, key_ref, value_ref, squares_ref, message_ref
):
    query = products(offsets, 0, blocks_ref, weight_ref, total_ref[...])
    rows = query.shape[0]
    held = query.shape[1] // HEAD_SIZE
    for target in range(message_ref.shape[0]):
        head, first = target * pairs // rows, target * pairs % rows
        slots = slice(first, first + pairs)
        columns = slice(head * HEAD_SIZE, (head + 1) * HEAD_SIZE)
        sent = range(head, held, KEY_VALUE_HEADS) if held % KEY_VALUE_HEADS == 0 else range(held)
        at = 0
        for j in sent:
            message_ref[target, at : at + pairs, :] = query[slots, j * HEAD_SIZE : (j + 1) * HEAD_SIZE]
            at += pairs
        message_ref[target, at : at + pairs, :] = key_ref[slots, columns]
        message_ref[target, at + pairs : at + 2 * pairs, :] = value_ref[slots, columns]
        message_ref[target, at + 2 * pairs : at + 3 * pairs, :] = squares_ref[slots, :]


def rotated(values, cosines, sines):
    even = lax.broadcasted_iota(jnp.int32, values.shape, 1) % 2 == 0
    swapped = jnp.where(
        even, -pltpu.roll(values, HEAD_SIZE - 1, 1), pltpu.roll(values, 1, 1)
    )
    return values * cosines + swapped * sines


def side_by_side(ref, members, start, size):
    parts = [ref[i, start : start + size, :] for i in members]
    return parts[0] if len(parts) == 1 else jnp.concatenate(parts, axis=1)


def folded(op, array):
    tiles = [array[:, at : at + HEAD_SIZE] for at in range(0, array.shape[1], HEAD_SIZE)]
    while len(tiles) > 1:
        tiles = [op(*tiles[k : k + 2]) if k + 1 < len(tiles) else tiles[k] for k in range(0, len(tiles), 2)]
    return tiles[0]


def attend_kernel(
    pairs, width, limits_ref, turns_ref, query_ref, rest_ref, keys_ref, values_ref, out_ref, scores_ref, wide_ref
):
    group = query_ref.shape[0]
    length = keys_ref.shape[1]
    at = rest_ref.shape[1] - 3 * pairs
    summed = jnp.sum(rest_ref[:, at:, :], axis=0)
    score_scale = 1.0 / math.sqrt(HEAD_SIZE)
    step = math.gcd(length, 512)
    many = 2 if pairs % 2 == 0 else 1
    parts = []
    for base in range(0, pairs, many):
        members = range(base, base + many)
        queries, owns, values, limits = [], [], [], []
        for i in members:
            scale = lax.rsqrt(summed[2 * pairs + i : 2 * pairs + i + 1, :] * (1.0 / width) + EPS)
            cosines, sines = turns_ref[0, i : i + 1, :], turns_ref[1, i : i + 1, :]
            query = rotated(query_ref[:, i, :] * scale, cosines, sines).astype(BF16)
            key = jnp.broadcast_to(summed[i : i + 1, :] * scale, (8, HEAD_SIZE))
            key = rotated(key, cosines, sines)[0:1, :].astype(BF16).astype(F32)
            values.append((summed[pairs + i : pairs + i + 1, :] * scale).astype(BF16).astype(F32))
            owns.append(jnp.sum(query.astype(F32) * key, axis=1, keepdims=True))
            limits.append(jnp.broadcast_to(limits_ref[i : i + 1, :], (group, HEAD_SIZE)))
            blank = jnp.zeros_like(query)
            queries.append(
                query
                if many == 1
                else jnp.concatenate([query if j == i else blank for j in members], axis=1)
            )
        stacked = jnp.concatenate(queries, axis=0)
        own = jnp.concatenate(owns, axis=0)
        limit = jnp.concatenate(limits, axis=0)
        column = lax.broadcasted_iota(jnp.int32, (many * group, HEAD_SIZE), 1)
        tops = jnp.broadcast_to(own, (many * group, HEAD_SIZE))
        place = base // many
        for start in range(0, length, step):
            scores = lax.dot_general(
                stacked,
                side_by_side(keys_ref, members, start, step),
                (((1,), (1,)), ((), ())),
                preferred_element_type=F32,
            )
            for at in range(0, step, HEAD_SIZE):
                tile = jnp.where(
                    column < limit - (start + at), scores[:, at : at + HEAD_SIZE], -jnp.inf
                )
                scores_ref[place, :, start + at : start + at + HEAD_SIZE] = tile
                tops = jnp.maximum(tops, tile)
        parts.append((members, place, own, tops, values))
    factor = score_scale * math.log2(math.e)
    for members, place, own, tops, values in parts:
        top = jnp.max(tops, axis=1, keepdims=True)
        own_w = jnp.exp2((own - top) * factor)
        sums = jnp.zeros_like(tops)
        blended = jnp.zeros((many * group, many * HEAD_SIZE), F32)
        for start in range(0, length, step):
            weights = jnp.exp2((scores_ref[place, :, start : start + step] - top) * factor)
            sums = sums + folded(jnp.add, weights)
            blended = blended + jnp.dot(
                weights.astype(BF16),
                side_by_side(values_ref, members, start, step),
                preferred_element_type=F32,
            )
        share = 1.0 / (own_w + jnp.sum(sums, axis=1, keepdims=True))
        blended = blended * share
        own_p = (own_w * share).astype(BF16).astype(F32)
        for k, i in enumerate(members):
            rows = slice(k * group, (k + 1) * group)
            result = blended[rows, k * HEAD_SIZE : (k + 1) * HEAD_SIZE] + own_p[rows] * values[k]
            for g in range(group):
                wide_ref[i : i + 1, g * HEAD_SIZE : (g + 1) * HEAD_SIZE] = result[g : g + 1, :]
    out_ref[...] = wide_ref[...].astype(BF16)


def project_half(pairs, head_offsets, slot_offsets, slot_ref, pieces, weight_ref, total):
    rows = slot_ref.shape[1]
    held = pieces[0].shape[1]
    devices_of_head = rows // pairs
    place = lax.axis_index("wide")
    group_place = place % devices_of_head
    head_place = place // devices_of_head
    slot_of_row = jnp.transpose(jnp.broadcast_to(slot_ref[...], (rows, rows)))[:, 0:1]
    position = lax.broadcasted_iota(jnp.int32, (rows, held), 1)
    picks = []
    for offsets in slot_offsets:
        device = jnp.zeros_like(position)
        for k, offset in enumerate(offsets):
            device = jnp.where(position // pairs == k, group_place ^ offset, device)
        picks.append((slot_of_row == device * pairs + position % pairs).astype(BF16))
    ordered = [
        sum(
            jnp.dot(pick, piece[z], preferred_element_type=F32) for pick, piece in zip(picks, pieces)
        ).astype(BF16)
        for z in range(len(head_offsets))
    ]
    for g in range(QUERY_GROUP):
        columns = slice(g * HEAD_SIZE, (g + 1) * HEAD_SIZE)
        weights = []
        for offset in head_offsets:
            start = (g * KEY_VALUE_HEADS + (head_place ^ offset)) * HEAD_SIZE
            weights.append(weight_ref[pl.ds(pl.multiple_of(start, HEAD_SIZE), HEAD_SIZE), :])
        total = total + jnp.dot(
            jnp.concatenate([o[:, columns] for o in ordered], axis=1),
            jnp.concatenate(weights, axis=0),
            preferred_element_type=F32,
        )
    return total


def first_half_kernel(pairs, head_offsets, slot_offsets, slot_ref, mine_ref, other_ref, weight_ref, out_ref):
    out_ref[...] = project_half(
        pairs,
        head_offsets,
        slot_offsets,
        slot_ref,
        (mine_ref, other_ref),
        weight_ref,
        jnp.zeros(out_ref.shape, F32),
    )


def second_half_kernel(
    pairs, head_offsets, slot_offsets, slot_ref, mine_ref, other_ref, weight_ref, half_ref, out_ref
):
    out_ref[...] = project_half(
        pairs, head_offsets, slot_offsets, slot_ref, (mine_ref, other_ref), weight_ref, half_ref[...]
    ).astype(BF16)


def swap(array, bit, count):
    return lax.ppermute(array, "wide", [(i, i ^ bit) for i in range(count)])


def body(
    count,
    tokens,
    norm_gain,
    slot_of_row,
    lengths,
    w_query,
    key_projection,
    value_projection,
    output_projection,
    slot_key_cache,
    slot_value_cache,
):
    rows, features = tokens.shape
    pairs = slot_key_cache.shape[0]
    width = w_query.shape[0]
    query_columns = w_query.shape[1]
    held = query_columns // HEAD_SIZE
    devices_of_head = rows // pairs
    bits = [1 << b for b in reversed(range(count.bit_length() - 1))]

    slot_row = slot_of_row.reshape(1, rows)
    scaled = call(
        prepare_kernel,
        jax.ShapeDtypeStruct((rows, features), BF16),
        (tokens, norm_gain, slot_row, w_query),
        far=(0, 1, 2, 3),
        scratch=(
            pltpu.VMEM((rows, features), BF16),
            pltpu.VMEM((features,), BF16),
            pltpu.VMEM((1, rows), jnp.int32),
            pltpu.SemaphoreType.DMA((3,)),
        ),
        read=8 * w_query.size,
    )
    index = np.arange(HEAD_SIZE)
    rate = (ROPE_BASE ** (-(index - index % 2) / HEAD_SIZE)).astype(np.float32)[None, :]
    totals = jax.ShapeDtypeStruct((rows, query_columns), F32)
    shares = jax.ShapeDtypeStruct((rows, key_projection.shape[1]), F32)

    def query(offsets, first, array, total):
        return call(
            functools.partial(query_kernel, tuple(offsets), first),
            totals,
            (array, w_query, total),
            near=(0, 1),
            flops=2 * rows * len(offsets) * features * query_columns,
            read=2 * len(offsets) * features * query_columns,
        )

    core, half = bits[-1], count // 2
    blocks, offsets, new, after = scaled[None], [0], [0], None
    for far in bits[:-1]:
        arrived = swap(blocks, far, count)
        if len(offsets) == 2:
            after, turns, limits = call(
                functools.partial(query_turns_kernel, tuple(offsets), pairs),
                (
                    totals,
                    jax.ShapeDtypeStruct((2, pairs, HEAD_SIZE), F32),
                    jax.ShapeDtypeStruct((pairs, HEAD_SIZE), jnp.int32),
                ),
                (blocks, w_query, lengths, jnp.asarray(rate)),
                near=(0, 1),
                smem=(2,),
                flops=2 * rows * len(offsets) * features * query_columns,
                read=2 * len(offsets) * features * query_columns,
            )
        elif len(offsets) > 2:
            after = query(new, len(offsets) - len(new), blocks, after)
        if len(offsets) == 4:
            key_share, value_share, squares = call(
                share_kernel,
                (shares, shares, jax.ShapeDtypeStruct((rows, HEAD_SIZE), F32)),
                (scaled, tokens, slot_row, key_projection, value_projection, after),
                near=(0,),
                far=(1, 2, 3, 4),
                scratch=(
                    pltpu.VMEM((rows, features), BF16),
                    pltpu.VMEM((1, rows), jnp.int32),
                    pltpu.VMEM(key_projection.shape, BF16),
                    pltpu.VMEM(value_projection.shape, BF16),
                    pltpu.SemaphoreType.DMA((4,)),
                ),
                flops=4 * rows * key_projection.size,
                read=4 * key_projection.size,
            )
        new = [o ^ far for o in offsets]
        if 2 * len(offsets) == half:
            break
        blocks = call(
            join_kernel,
            jax.ShapeDtypeStruct((2 * len(offsets), rows, features), BF16),
            (blocks, arrived) if after is None else (blocks, arrived, key_share if len(offsets) == 4 else after),
        )
        offsets = offsets + new
    blocks = call(
        pass_kernel, jax.ShapeDtypeStruct(blocks.shape, BF16), (blocks, arrived, after, key_share)
    )
    first = swap(blocks, core, count)
    last = swap(arrived, core, count)
    total = query(new, 0, arrived, after)
    total = query([o ^ core for o in offsets], 0, first, total)
    sent = held // KEY_VALUE_HEADS if held % KEY_VALUE_HEADS == 0 else held
    message = call(
        functools.partial(message_kernel, tuple(o ^ core for o in new), pairs),
        jax.ShapeDtypeStruct((count, pairs * (sent + 3), HEAD_SIZE), F32),
        (last, w_query, total, key_share, value_share, squares),
        near=(0, 1),
        flops=2 * last.size * query_columns,
        read=2 * len(new) * features * query_columns,
    )

    got = lax.all_to_all(message, "wide", 0, 0, tiled=True)
    if sent == 1 and held % KEY_VALUE_HEADS == 0:
        query_rows = got
    else:
        query_rows = (
            got[:, : pairs * sent].reshape(count, sent, pairs, HEAD_SIZE).reshape(-1, pairs, HEAD_SIZE)
        )
        if held % KEY_VALUE_HEADS:
            head = lax.axis_index("wide") // devices_of_head
            query_rows = lax.dynamic_index_in_dim(
                query_rows.reshape(QUERY_GROUP, KEY_VALUE_HEADS, pairs, HEAD_SIZE), head, 1, False
            )
    cache_bytes = 2 * slot_key_cache.size
    attended = call(
        functools.partial(attend_kernel, pairs, width),
        jax.ShapeDtypeStruct((pairs, QUERY_GROUP * HEAD_SIZE), BF16),
        (limits, turns, query_rows, got, slot_key_cache, slot_value_cache),
        near=(4, 5),
        scratch=(
            pltpu.VMEM(
                ((pairs + 1) // 2, min(pairs, 2) * QUERY_GROUP, slot_key_cache.shape[1]), F32
            ),
            pltpu.VMEM((pairs, QUERY_GROUP * HEAD_SIZE), F32),
        ),
        limit=8 * MIB,
        flops=4 * QUERY_GROUP * slot_key_cache.size,
        read=2 * cache_bytes,
    )

    mine = attended[None]
    slot_offsets = [0]
    for far in bits:
        if core < far < devices_of_head:
            mine = jnp.concatenate([mine, swap(mine, far, count)], 1)
            slot_offsets = slot_offsets + [o ^ far for o in slot_offsets]
    high, low = bits[0] // devices_of_head, bits[1] // devices_of_head
    mine = jnp.concatenate([mine, swap(mine, bits[0], count)], 0)
    across = swap(mine, bits[1], count)
    beside = swap(mine, core, count)
    slots = (tuple(slot_offsets), tuple(o ^ core for o in slot_offsets))
    columns = output_projection.shape[1]
    half = call(
        functools.partial(first_half_kernel, pairs, (0, high), slots),
        jax.ShapeDtypeStruct((rows, columns), F32),
        (slot_row, mine, beside, output_projection),
        near=(3,),
        flops=rows * output_projection.size,
        read=output_projection.size,
    )
    across = call(pass_kernel, jax.ShapeDtypeStruct(across.shape, BF16), (across, half))
    both = swap(across, core, count)
    return call(
        functools.partial(second_half_kernel, pairs, (low, low ^ high), slots),
        jax.ShapeDtypeStruct((rows, columns), BF16),
        (slot_row, across, both, output_projection, half),
        near=(3,),
        flops=rows * output_projection.size,
        read=output_projection.size,
    )


def solution(mesh):
    placed = (
        P("groups", "wide"),
        P("wide"),
        P("groups"),
        P("groups"),
        P(None, "wide"),
        P("wide", None),
        P("wide", None),
        P(None, "wide"),
        P(("groups", "wide"), None, None),
        P(("groups", "wide"), None, None),
    )
    return jax.shard_map(
        functools.partial(body, mesh.shape["wide"]),
        mesh=mesh,
        in_specs=placed,
        out_specs=P("groups", "wide"),
        check_vma=False,
    )
```

```python
import functools
import math

import jax
import jax.numpy as jnp
import numpy as np
from jax import lax
from jax.experimental import pallas as pl
from jax.experimental.pallas import tpu as pltpu
from jax.sharding import PartitionSpec as P

QUERY_HEADS = 64
KEY_VALUE_HEADS = 4
HEAD_SIZE = 128
QUERY_GROUP = QUERY_HEADS // KEY_VALUE_HEADS

EPS = 1e-05
ROPE_BASE = 500000.0
MIB = 1 << 20
F32 = jnp.float32
BF16 = jnp.bfloat16


def call(kernel, out_shape, args, near=(), far=(), smem=(), scratch=(), limit=4 * MIB, flops=0, read=0):
    operands, specs = [], []
    for i, arg in enumerate(args):
        space = pltpu.SMEM if i in smem else pltpu.VMEM
        if i in near:
            arg = pltpu.with_memory_space_constraint(arg, pltpu.VMEM)
        if i in far:
            arg = pltpu.with_memory_space_constraint(arg, pltpu.HBM)
            space = pltpu.HBM
        operands.append(arg)
        specs.append(pl.BlockSpec(memory_space=space))
    return pl.pallas_call(
        kernel,
        out_shape=out_shape,
        in_specs=specs,
        out_specs=jax.tree.map(lambda _: pl.BlockSpec(memory_space=pltpu.VMEM), out_shape),
        scratch_shapes=list(scratch),
        compiler_params=pltpu.CompilerParams(vmem_limit_bytes=limit),
        cost_estimate=pl.CostEstimate(flops=flops, bytes_accessed=read, transcendentals=0),
    )(*operands)


def fetch(pairs, sems):
    copies = [pltpu.make_async_copy(far, near, sems.at[i]) for i, (far, near) in enumerate(pairs)]
    for copy in copies:
        copy.start()
    return copies


def picked_rows(slot_ref):
    rows = slot_ref.shape[1]
    return lax.broadcasted_iota(jnp.int32, (rows, rows), 0) == slot_ref[...]


def prepare_kernel(
    far_tokens, far_gain, far_slot, far_query, scaled_ref, tokens_ref, gain_ref, slot_ref, sems
):
    for copy in fetch(((far_tokens, tokens_ref), (far_gain, gain_ref), (far_slot, slot_ref)), sems):
        copy.wait()
    gain = gain_ref[...].astype(F32).reshape(1, gain_ref.shape[0])
    scaled = (tokens_ref[...].astype(F32) * gain).astype(BF16)
    scaled_ref[...] = jnp.dot(
        picked_rows(slot_ref).astype(BF16), scaled, preferred_element_type=F32
    ).astype(BF16)


def pass_kernel(array_ref, *refs):
    refs[-1][...] = array_ref[...]


def join_kernel(mine_ref, arrived_ref, *refs):
    joined_ref = refs[-1]
    count = mine_ref.shape[0]
    joined_ref[:count] = mine_ref[...]
    joined_ref[count:] = arrived_ref[...]


def share_kernel(
    pairs,
    scaled_ref,
    lengths_ref,
    rate_ref,
    far_tokens,
    far_slot,
    far_key,
    far_value,
    key_share_ref,
    value_share_ref,
    squares_ref,
    turns_ref,
    limits_ref,
    tokens_ref,
    slot_ref,
    key_ref,
    value_ref,
    sems,
):
    copies = fetch(
        ((far_tokens, tokens_ref), (far_slot, slot_ref), (far_key, key_ref), (far_value, value_ref)), sems
    )
    own = (lax.axis_index("wide") * pairs) % lengths_ref.shape[0]
    positions = jnp.concatenate(
        [jnp.full((1, HEAD_SIZE), lengths_ref[own + i], jnp.int32) for i in range(pairs)], 0
    )
    angle = positions.astype(F32) * rate_ref[...]
    turns_ref[0] = jnp.cos(angle)
    turns_ref[1] = jnp.sin(angle)
    limits_ref[...] = positions
    copies[0].wait()
    copies[1].wait()
    rows = tokens_ref.shape[0]
    wide_f = tokens_ref[...].astype(F32)
    squares = jnp.sum(wide_f * wide_f, axis=1, keepdims=True)
    turned = jnp.transpose(jnp.broadcast_to(squares, (rows, rows)))
    squares = jnp.sum(jnp.where(picked_rows(slot_ref), turned, 0.0), axis=1, keepdims=True)
    squares_ref[...] = jnp.broadcast_to(squares, squares_ref.shape)
    copies[2].wait()
    key_share_ref[...] = jnp.dot(scaled_ref[...], key_ref[...], preferred_element_type=F32)
    copies[3].wait()
    value_share_ref[...] = jnp.dot(scaled_ref[...], value_ref[...], preferred_element_type=F32)


def products(offsets, pieces, weight_ref, total):
    place = lax.axis_index("wide")
    for of_piece, blocks_ref in zip(offsets, pieces):
        features = blocks_ref.shape[2]
        for k, offset in enumerate(of_piece):
            start = pl.multiple_of((place ^ offset) * features, features)
            total = total + jnp.dot(
                blocks_ref[k], weight_ref[pl.ds(start, features), :], preferred_element_type=F32
            )
    return total


def query_kernel(offsets, weight_ref, *refs):
    pieces, before, out_ref = refs[: len(offsets)], refs[len(offsets) : -1], refs[-1]
    total = before[0][...] if before else jnp.zeros(out_ref.shape, F32)
    out_ref[...] = products(offsets, pieces, weight_ref, total)


def message_kernel(offsets, pairs, weight_ref, total_ref, key_ref, value_ref, squares_ref, *refs):
    message_ref = refs[-1]
    query = products(offsets, refs[:-1], weight_ref, total_ref[...])
    rows = query.shape[0]
    held = query.shape[1] // HEAD_SIZE
    for target in range(message_ref.shape[0]):
        head, first = target * pairs // rows, target * pairs % rows
        slots = slice(first, first + pairs)
        columns = slice(head * HEAD_SIZE, (head + 1) * HEAD_SIZE)
        sent = range(head, held, KEY_VALUE_HEADS) if held % KEY_VALUE_HEADS == 0 else range(held)
        at = 0
        for j in sent:
            message_ref[target, at : at + pairs, :] = query[slots, j * HEAD_SIZE : (j + 1) * HEAD_SIZE]
            at += pairs
        message_ref[target, at : at + pairs, :] = key_ref[slots, columns]
        message_ref[target, at + pairs : at + 2 * pairs, :] = value_ref[slots, columns]
        message_ref[target, at + 2 * pairs : at + 3 * pairs, :] = squares_ref[slots, :]


def rotated(values, cosines, sines):
    even = lax.broadcasted_iota(jnp.int32, values.shape, 1) % 2 == 0
    swapped = jnp.where(
        even, -pltpu.roll(values, HEAD_SIZE - 1, 1), pltpu.roll(values, 1, 1)
    )
    return values * cosines + swapped * sines


def side_by_side(ref, members, start, size):
    parts = [ref[i, start : start + size, :] for i in members]
    return parts[0] if len(parts) == 1 else jnp.concatenate(parts, axis=1)


def folded(op, array):
    tiles = [array[:, at : at + HEAD_SIZE] for at in range(0, array.shape[1], HEAD_SIZE)]
    while len(tiles) > 1:
        tiles = [op(*tiles[k : k + 2]) if k + 1 < len(tiles) else tiles[k] for k in range(0, len(tiles), 2)]
    return tiles[0]


def attend_kernel(
    pairs, width, limits_ref, turns_ref, query_ref, rest_ref, keys_ref, values_ref, out_ref, scores_ref, wide_ref
):
    group = query_ref.shape[0]
    length = keys_ref.shape[1]
    at = rest_ref.shape[1] - 3 * pairs
    summed = jnp.sum(rest_ref[:, at:, :], axis=0)
    score_scale = 1.0 / math.sqrt(HEAD_SIZE)
    step = math.gcd(length, 512)
    many = 2 if pairs % 2 == 0 else 1
    parts = []
    for base in range(0, pairs, many):
        members = range(base, base + many)
        queries, owns, values, limits = [], [], [], []
        for i in members:
            scale = lax.rsqrt(summed[2 * pairs + i : 2 * pairs + i + 1, :] * (1.0 / width) + EPS)
            cosines, sines = turns_ref[0, i : i + 1, :], turns_ref[1, i : i + 1, :]
            query = rotated(query_ref[:, i, :] * scale, cosines, sines).astype(BF16)
            key = jnp.broadcast_to(summed[i : i + 1, :] * scale, (8, HEAD_SIZE))
            key = rotated(key, cosines, sines)[0:1, :].astype(BF16).astype(F32)
            values.append((summed[pairs + i : pairs + i + 1, :] * scale).astype(BF16).astype(F32))
            owns.append(jnp.sum(query.astype(F32) * key, axis=1, keepdims=True))
            limits.append(jnp.broadcast_to(limits_ref[i : i + 1, :], (group, HEAD_SIZE)))
            blank = jnp.zeros_like(query)
            queries.append(
                query
                if many == 1
                else jnp.concatenate([query if j == i else blank for j in members], axis=1)
            )
        stacked = jnp.concatenate(queries, axis=0)
        own = jnp.concatenate(owns, axis=0)
        limit = jnp.concatenate(limits, axis=0)
        column = lax.broadcasted_iota(jnp.int32, (many * group, HEAD_SIZE), 1)
        tops = jnp.broadcast_to(own, (many * group, HEAD_SIZE))
        place = base // many
        for start in range(0, length, step):
            scores = lax.dot_general(
                stacked,
                side_by_side(keys_ref, members, start, step),
                (((1,), (1,)), ((), ())),
                preferred_element_type=F32,
            )
            for at in range(0, step, HEAD_SIZE):
                tile = jnp.where(
                    column < limit - (start + at), scores[:, at : at + HEAD_SIZE], -jnp.inf
                )
                scores_ref[place, :, start + at : start + at + HEAD_SIZE] = tile
                tops = jnp.maximum(tops, tile)
        parts.append((members, place, own, tops, values))
    factor = score_scale * math.log2(math.e)
    for members, place, own, tops, values in parts:
        top = jnp.max(tops, axis=1, keepdims=True)
        own_w = jnp.exp2((own - top) * factor)
        sums = jnp.zeros_like(tops)
        blended = jnp.zeros((many * group, many * HEAD_SIZE), F32)
        for start in range(0, length, step):
            weights = jnp.exp2((scores_ref[place, :, start : start + step] - top) * factor)
            sums = sums + folded(jnp.add, weights)
            blended = blended + jnp.dot(
                weights.astype(BF16),
                side_by_side(values_ref, members, start, step),
                preferred_element_type=F32,
            )
        share = 1.0 / (own_w + jnp.sum(sums, axis=1, keepdims=True))
        blended = blended * share
        own_p = (own_w * share).astype(BF16).astype(F32)
        for k, i in enumerate(members):
            rows = slice(k * group, (k + 1) * group)
            result = blended[rows, k * HEAD_SIZE : (k + 1) * HEAD_SIZE] + own_p[rows] * values[k]
            for g in range(group):
                wide_ref[i : i + 1, g * HEAD_SIZE : (g + 1) * HEAD_SIZE] = result[g : g + 1, :]
    out_ref[...] = wide_ref[...].astype(BF16)


def project_half(pairs, places, slot_ref, pieces, weight_ref, total):
    rows = slot_ref.shape[1]
    held = pieces[0].shape[1]
    devices_of_head = rows // pairs
    place = lax.axis_index("wide")
    slot_of_row = jnp.transpose(jnp.broadcast_to(slot_ref[...], (rows, rows)))[:, 0:1]
    position = lax.broadcasted_iota(jnp.int32, (rows, held), 1)
    ordered, heads = [], []
    for z, by_piece in enumerate(places):
        result = 0.0
        for offsets, piece in zip(by_piece, pieces):
            device = jnp.zeros_like(position)
            for k, offset in enumerate(offsets):
                device = jnp.where(position // pairs == k, (place ^ offset) % devices_of_head, device)
            pick = (slot_of_row == device * pairs + position % pairs).astype(BF16)
            result = result + jnp.dot(pick, piece[z], preferred_element_type=F32)
        ordered.append(result.astype(BF16))
        heads.append((place ^ by_piece[0][0]) // devices_of_head)
    for g in range(QUERY_GROUP):
        columns = slice(g * HEAD_SIZE, (g + 1) * HEAD_SIZE)
        weights = []
        for head in heads:
            start = pl.multiple_of((g * KEY_VALUE_HEADS + head) * HEAD_SIZE, HEAD_SIZE)
            weights.append(weight_ref[pl.ds(start, HEAD_SIZE), :])
        total = total + jnp.dot(
            jnp.concatenate([o[:, columns] for o in ordered], axis=1),
            jnp.concatenate(weights, axis=0),
            preferred_element_type=F32,
        )
    return total


def first_half_kernel(pairs, places, slot_ref, weight_ref, *refs):
    out_ref = refs[-1]
    out_ref[...] = project_half(
        pairs, places, slot_ref, refs[:-1], weight_ref, jnp.zeros(out_ref.shape, F32)
    )


def second_half_kernel(pairs, places, slot_ref, weight_ref, half_ref, *refs):
    out_ref = refs[-1]
    out_ref[...] = project_half(pairs, places, slot_ref, refs[:-1], weight_ref, half_ref[...]).astype(BF16)


def passed(array, *after):
    return call(pass_kernel, jax.ShapeDtypeStruct(array.shape, array.dtype), (array, *after))


def swap(array, bit, count):
    return lax.ppermute(array, "wide", [(i, i ^ bit) for i in range(count)])


def body(
    count,
    tokens,
    norm_gain,
    slot_of_row,
    lengths,
    w_query,
    key_projection,
    value_projection,
    output_projection,
    slot_key_cache,
    slot_value_cache,
):
    rows, features = tokens.shape
    pairs = slot_key_cache.shape[0]
    width = w_query.shape[0]
    query_columns = w_query.shape[1]
    held = query_columns // HEAD_SIZE
    devices_of_head = rows // pairs
    bits = [1 << b for b in reversed(range(count.bit_length() - 1))]

    slot_row = slot_of_row.reshape(1, rows)
    scaled = call(
        prepare_kernel,
        jax.ShapeDtypeStruct((rows, features), BF16),
        (tokens, norm_gain, slot_row, w_query),
        far=(0, 1, 2, 3),
        scratch=(
            pltpu.VMEM((rows, features), BF16),
            pltpu.VMEM((features,), BF16),
            pltpu.VMEM((1, rows), jnp.int32),
            pltpu.SemaphoreType.DMA((3,)),
        ),
        read=8 * w_query.size,
    )
    index = np.arange(HEAD_SIZE)
    rate = (ROPE_BASE ** (-(index - index % 2) / HEAD_SIZE)).astype(np.float32)[None, :]
    totals = jax.ShapeDtypeStruct((rows, query_columns), F32)
    shares = jax.ShapeDtypeStruct((rows, key_projection.shape[1]), F32)

    def query(by_piece, *total):
        blocks = sum(piece.shape[0] for piece in by_piece.values())
        return call(
            functools.partial(query_kernel, tuple(tuple(o ^ by for o in offsets) for by in by_piece)),
            totals,
            (w_query, *by_piece.values(), *total),
            near=range(1 + len(by_piece)),
            flops=2 * rows * blocks * features * query_columns,
            read=2 * blocks * features * query_columns,
        )

    *outer, far, near, core = bits
    corners = (far | near | core, near | core, far | core)
    blocks, offsets, key_share = scaled[None], [0], None
    for bit in outer:
        arrived = swap(blocks, bit | core, count)
        if key_share is None:
            key_share, value_share, squares, turns, limits = call(
                functools.partial(share_kernel, pairs),
                (
                    shares,
                    shares,
                    jax.ShapeDtypeStruct((rows, HEAD_SIZE), F32),
                    jax.ShapeDtypeStruct((2, pairs, HEAD_SIZE), F32),
                    jax.ShapeDtypeStruct((pairs, HEAD_SIZE), jnp.int32),
                ),
                (scaled, lengths, jnp.asarray(rate), tokens, slot_row, key_projection, value_projection),
                near=(0,),
                far=(3, 4, 5, 6),
                smem=(1,),
                scratch=(
                    pltpu.VMEM((rows, features), BF16),
                    pltpu.VMEM((1, rows), jnp.int32),
                    pltpu.VMEM(key_projection.shape, BF16),
                    pltpu.VMEM(value_projection.shape, BF16),
                    pltpu.SemaphoreType.DMA((4,)),
                ),
                flops=4 * rows * key_projection.size,
                read=4 * key_projection.size,
            )
        blocks = call(
            join_kernel,
            jax.ShapeDtypeStruct((2 * len(offsets), rows, features), BF16),
            (blocks, arrived, key_share),
        )
        offsets = offsets + [o ^ bit ^ core for o in offsets]
    pieces = {by: swap(blocks, by, count) for by in corners}
    total = query({0: blocks, core: swap(blocks, core, count)})
    pieces = {by: passed(piece, total) for by, piece in pieces.items()}
    last = {by ^ core: swap(piece, core, count) for by, piece in pieces.items()}
    total = query(pieces, total)
    sent = held // KEY_VALUE_HEADS if held % KEY_VALUE_HEADS == 0 else held
    message = call(
        functools.partial(
            message_kernel, tuple(tuple(o ^ by for o in offsets) for by in last), pairs
        ),
        jax.ShapeDtypeStruct((count, pairs * (sent + 3), HEAD_SIZE), F32),
        (w_query, total, key_share, value_share, squares, *last.values()),
        near=(0, *range(5, 5 + len(last))),
        flops=6 * blocks.size * query_columns,
        read=6 * len(offsets) * features * query_columns,
    )

    got = lax.all_to_all(message, "wide", 0, 0, tiled=True)
    if sent == 1 and held % KEY_VALUE_HEADS == 0:
        query_rows = got
    else:
        query_rows = (
            got[:, : pairs * sent].reshape(count, sent, pairs, HEAD_SIZE).reshape(-1, pairs, HEAD_SIZE)
        )
        if held % KEY_VALUE_HEADS:
            head = lax.axis_index("wide") // devices_of_head
            query_rows = lax.dynamic_index_in_dim(
                query_rows.reshape(QUERY_GROUP, KEY_VALUE_HEADS, pairs, HEAD_SIZE), head, 1, False
            )
    cache_bytes = 2 * slot_key_cache.size
    attended = call(
        functools.partial(attend_kernel, pairs, width),
        jax.ShapeDtypeStruct((pairs, QUERY_GROUP * HEAD_SIZE), BF16),
        (limits, turns, query_rows, got, slot_key_cache, slot_value_cache),
        near=(4, 5),
        scratch=(
            pltpu.VMEM(
                ((pairs + 1) // 2, min(pairs, 2) * QUERY_GROUP, slot_key_cache.shape[1]), F32
            ),
            pltpu.VMEM((pairs, QUERY_GROUP * HEAD_SIZE), F32),
        ),
        limit=8 * MIB,
        flops=4 * QUERY_GROUP * slot_key_cache.size,
        read=2 * cache_bytes,
    )

    mine = attended[None]
    offsets = [0]
    for bit in bits:
        if near < bit < devices_of_head:
            mine = jnp.concatenate([mine, swap(mine, bit | core, count)], 1)
            offsets = offsets + [o ^ bit ^ core for o in offsets]
    high, low = bits[0] | core, bits[1]
    mine = jnp.concatenate([mine, swap(mine, high, count)], 0)
    corners = (near | core, low | near | core, low | core)
    pieces = {0: mine} | {by: swap(mine, by, count) for by in corners}

    def with_core(*members):
        both = [(by, pieces[by]) for by in members]
        both += [(by ^ core, swap(pieces[by], core, count)) for by in members]
        places = tuple(
            tuple(tuple(o ^ head ^ by for o in offsets) for by, _ in both) for head in (0, high)
        )
        return places, [piece for _, piece in both]

    columns = output_projection.shape[1]
    places, held_pieces = with_core(0, corners[0])
    half = call(
        functools.partial(first_half_kernel, pairs, places),
        jax.ShapeDtypeStruct((rows, columns), F32),
        (slot_row, output_projection, *held_pieces),
        near=(1,),
    )
    places, held_pieces = with_core(*corners[1:])
    return call(
        functools.partial(second_half_kernel, pairs, places),
        jax.ShapeDtypeStruct((rows, columns), BF16),
        (slot_row, output_projection, half, *held_pieces),
        near=(1,),
        flops=rows * output_projection.size,
        read=output_projection.size,
    )


def solution(mesh):
    placed = (
        P("groups", "wide"),
        P("wide"),
        P("groups"),
        P("groups"),
        P(None, "wide"),
        P("wide", None),
        P("wide", None),
        P(None, "wide"),
        P(("groups", "wide"), None, None),
        P(("groups", "wide"), None, None),
    )
    return jax.shard_map(
        functools.partial(body, mesh.shape["wide"]),
        mesh=mesh,
        in_specs=placed,
        out_specs=P("groups", "wide"),
        check_vma=False,
    )
```

```python
import functools
import math

import jax
import jax.numpy as jnp
import numpy as np
from jax import lax
from jax.experimental import pallas as pl
from jax.experimental.pallas import tpu as pltpu
from jax.sharding import PartitionSpec as P

QUERY_HEADS = 64
KEY_VALUE_HEADS = 4
HEAD_SIZE = 128
QUERY_GROUP = QUERY_HEADS // KEY_VALUE_HEADS

EPS = 1e-05
ROPE_BASE = 500000.0
MIB = 1 << 20
F32 = jnp.float32
BF16 = jnp.bfloat16


def call(kernel, out_shape, args, near=(), far=(), smem=(), scratch=(), limit=4 * MIB, flops=0, read=0):
    operands, specs = [], []
    for i, arg in enumerate(args):
        space = pltpu.SMEM if i in smem else pltpu.VMEM
        if i in near:
            arg = pltpu.with_memory_space_constraint(arg, pltpu.VMEM)
        if i in far:
            arg = pltpu.with_memory_space_constraint(arg, pltpu.HBM)
            space = pltpu.HBM
        operands.append(arg)
        specs.append(pl.BlockSpec(memory_space=space))
    return pl.pallas_call(
        kernel,
        out_shape=out_shape,
        in_specs=specs,
        out_specs=jax.tree.map(lambda _: pl.BlockSpec(memory_space=pltpu.VMEM), out_shape),
        scratch_shapes=list(scratch),
        compiler_params=pltpu.CompilerParams(vmem_limit_bytes=limit),
        cost_estimate=pl.CostEstimate(flops=flops, bytes_accessed=read, transcendentals=0),
    )(*operands)


def fetch(pairs, sems):
    copies = [pltpu.make_async_copy(far, near, sems.at[i]) for i, (far, near) in enumerate(pairs)]
    for copy in copies:
        copy.start()
    return copies


def picked_rows(slot_ref):
    rows = slot_ref.shape[1]
    return lax.broadcasted_iota(jnp.int32, (rows, rows), 0) == slot_ref[...]


def prepare_kernel(
    far_tokens, far_gain, far_slot, far_query, scaled_ref, tokens_ref, gain_ref, slot_ref, sems
):
    for copy in fetch(((far_tokens, tokens_ref), (far_gain, gain_ref), (far_slot, slot_ref)), sems):
        copy.wait()
    gain = gain_ref[...].astype(F32).reshape(1, gain_ref.shape[0])
    scaled = (tokens_ref[...].astype(F32) * gain).astype(BF16)
    scaled_ref[...] = jnp.dot(
        picked_rows(slot_ref).astype(BF16), scaled, preferred_element_type=F32
    ).astype(BF16)


def pass_kernel(array_ref, *refs):
    refs[-1][...] = array_ref[...]


def join_kernel(*refs):
    at = 0
    for ref in refs[:-2]:
        refs[-1][at : at + ref.shape[0]] = ref[...]
        at += ref.shape[0]


def share_kernel(
    pairs,
    scaled_ref,
    lengths_ref,
    rate_ref,
    far_tokens,
    far_slot,
    far_key,
    far_value,
    key_share_ref,
    value_share_ref,
    squares_ref,
    turns_ref,
    limits_ref,
    tokens_ref,
    slot_ref,
    key_ref,
    value_ref,
    sems,
):
    copies = fetch(
        ((far_tokens, tokens_ref), (far_slot, slot_ref), (far_key, key_ref), (far_value, value_ref)), sems
    )
    own = (lax.axis_index("wide") * pairs) % lengths_ref.shape[0]
    positions = jnp.concatenate(
        [jnp.full((1, HEAD_SIZE), lengths_ref[own + i], jnp.int32) for i in range(pairs)], 0
    )
    angle = positions.astype(F32) * rate_ref[...]
    turns_ref[0] = jnp.cos(angle)
    turns_ref[1] = jnp.sin(angle)
    limits_ref[...] = positions
    copies[0].wait()
    copies[1].wait()
    rows = tokens_ref.shape[0]
    wide_f = tokens_ref[...].astype(F32)
    squares = jnp.sum(wide_f * wide_f, axis=1, keepdims=True)
    turned = jnp.transpose(jnp.broadcast_to(squares, (rows, rows)))
    squares = jnp.sum(jnp.where(picked_rows(slot_ref), turned, 0.0), axis=1, keepdims=True)
    squares_ref[...] = jnp.broadcast_to(squares, squares_ref.shape)
    copies[2].wait()
    key_share_ref[...] = jnp.dot(scaled_ref[...], key_ref[...], preferred_element_type=F32)
    copies[3].wait()
    value_share_ref[...] = jnp.dot(scaled_ref[...], value_ref[...], preferred_element_type=F32)


def products(offsets, pieces, weight_ref, total):
    place = lax.axis_index("wide")
    blocks = [(ref, k) for ref in pieces for k in range(ref.shape[0])]
    for offset, (ref, k) in zip(offsets, blocks):
        features = ref.shape[2]
        start = pl.multiple_of((place ^ offset) * features, features)
        total = total + jnp.dot(
            ref[k], weight_ref[pl.ds(start, features), :], preferred_element_type=F32
        )
    return total


def query_kernel(offsets, count, weight_ref, *refs):
    pieces, before, out_ref = refs[:count], refs[count:-1], refs[-1]
    total = before[0][...] if before else jnp.zeros(out_ref.shape, F32)
    out_ref[...] = products(offsets, pieces, weight_ref, total)


def message_kernel(offsets, pairs, weight_ref, total_ref, key_ref, value_ref, squares_ref, *refs):
    message_ref = refs[-1]
    query = products(offsets, refs[:-1], weight_ref, total_ref[...])
    rows = query.shape[0]
    held = query.shape[1] // HEAD_SIZE
    for target in range(message_ref.shape[0]):
        head, first = target * pairs // rows, target * pairs % rows
        slots = slice(first, first + pairs)
        columns = slice(head * HEAD_SIZE, (head + 1) * HEAD_SIZE)
        sent = range(head, held, KEY_VALUE_HEADS) if held % KEY_VALUE_HEADS == 0 else range(held)
        at = 0
        for j in sent:
            message_ref[target, at : at + pairs, :] = query[slots, j * HEAD_SIZE : (j + 1) * HEAD_SIZE]
            at += pairs
        message_ref[target, at : at + pairs, :] = key_ref[slots, columns]
        message_ref[target, at + pairs : at + 2 * pairs, :] = value_ref[slots, columns]
        message_ref[target, at + 2 * pairs : at + 3 * pairs, :] = squares_ref[slots, :]


def rotated(values, cosines, sines):
    even = lax.broadcasted_iota(jnp.int32, values.shape, 1) % 2 == 0
    swapped = jnp.where(
        even, -pltpu.roll(values, HEAD_SIZE - 1, 1), pltpu.roll(values, 1, 1)
    )
    return values * cosines + swapped * sines


def side_by_side(ref, members, start, size):
    parts = [ref[i, start : start + size, :] for i in members]
    return parts[0] if len(parts) == 1 else jnp.concatenate(parts, axis=1)


def folded(op, array):
    tiles = [array[:, at : at + HEAD_SIZE] for at in range(0, array.shape[1], HEAD_SIZE)]
    while len(tiles) > 1:
        tiles = [op(*tiles[k : k + 2]) if k + 1 < len(tiles) else tiles[k] for k in range(0, len(tiles), 2)]
    return tiles[0]


def attend_kernel(
    pairs, width, limits_ref, turns_ref, query_ref, rest_ref, keys_ref, values_ref, out_ref, scores_ref, wide_ref
):
    group = query_ref.shape[0]
    length = keys_ref.shape[1]
    at = rest_ref.shape[1] - 3 * pairs
    summed = jnp.sum(rest_ref[:, at:, :], axis=0)
    score_scale = 1.0 / math.sqrt(HEAD_SIZE)
    step = math.gcd(length, 512)
    many = 2 if pairs % 2 == 0 else 1
    parts = []
    for base in range(0, pairs, many):
        members = range(base, base + many)
        queries, owns, values, limits = [], [], [], []
        for i in members:
            scale = lax.rsqrt(summed[2 * pairs + i : 2 * pairs + i + 1, :] * (1.0 / width) + EPS)
            cosines, sines = turns_ref[0, i : i + 1, :], turns_ref[1, i : i + 1, :]
            query = rotated(query_ref[:, i, :] * scale, cosines, sines).astype(BF16)
            key = jnp.broadcast_to(summed[i : i + 1, :] * scale, (8, HEAD_SIZE))
            key = rotated(key, cosines, sines)[0:1, :].astype(BF16).astype(F32)
            values.append((summed[pairs + i : pairs + i + 1, :] * scale).astype(BF16).astype(F32))
            owns.append(jnp.sum(query.astype(F32) * key, axis=1, keepdims=True))
            limits.append(jnp.broadcast_to(limits_ref[i : i + 1, :], (group, HEAD_SIZE)))
            blank = jnp.zeros_like(query)
            queries.append(
                query
                if many == 1
                else jnp.concatenate([query if j == i else blank for j in members], axis=1)
            )
        stacked = jnp.concatenate(queries, axis=0)
        own = jnp.concatenate(owns, axis=0)
        limit = jnp.concatenate(limits, axis=0)
        column = lax.broadcasted_iota(jnp.int32, (many * group, HEAD_SIZE), 1)
        tops = jnp.broadcast_to(own, (many * group, HEAD_SIZE))
        place = base // many
        for start in range(0, length, step):
            scores = lax.dot_general(
                stacked,
                side_by_side(keys_ref, members, start, step),
                (((1,), (1,)), ((), ())),
                preferred_element_type=F32,
            )
            for at in range(0, step, HEAD_SIZE):
                tile = jnp.where(
                    column < limit - (start + at), scores[:, at : at + HEAD_SIZE], -jnp.inf
                )
                scores_ref[place, :, start + at : start + at + HEAD_SIZE] = tile
                tops = jnp.maximum(tops, tile)
        parts.append((members, place, own, tops, values))
    factor = score_scale * math.log2(math.e)
    for members, place, own, tops, values in parts:
        top = jnp.max(tops, axis=1, keepdims=True)
        own_w = jnp.exp2((own - top) * factor)
        sums = jnp.zeros_like(tops)
        blended = jnp.zeros((many * group, many * HEAD_SIZE), F32)
        for start in range(0, length, step):
            weights = jnp.exp2((scores_ref[place, :, start : start + step] - top) * factor)
            sums = sums + folded(jnp.add, weights)
            blended = blended + jnp.dot(
                weights.astype(BF16),
                side_by_side(values_ref, members, start, step),
                preferred_element_type=F32,
            )
        share = 1.0 / (own_w + jnp.sum(sums, axis=1, keepdims=True))
        blended = blended * share
        own_p = (own_w * share).astype(BF16).astype(F32)
        for k, i in enumerate(members):
            rows = slice(k * group, (k + 1) * group)
            result = blended[rows, k * HEAD_SIZE : (k + 1) * HEAD_SIZE] + own_p[rows] * values[k]
            for g in range(group):
                wide_ref[i : i + 1, g * HEAD_SIZE : (g + 1) * HEAD_SIZE] = result[g : g + 1, :]
    out_ref[...] = wide_ref[...].astype(BF16)


def project_half(pairs, places, slot_ref, pieces, weight_ref, total):
    rows = slot_ref.shape[1]
    held = pieces[0].shape[1]
    devices_of_head = rows // pairs
    place = lax.axis_index("wide")
    slot_of_row = jnp.transpose(jnp.broadcast_to(slot_ref[...], (rows, rows)))[:, 0:1]
    position = lax.broadcasted_iota(jnp.int32, (rows, held), 1)
    ordered, heads = [], []
    for z, by_piece in enumerate(places):
        result = 0.0
        for offsets, piece in zip(by_piece, pieces):
            device = jnp.zeros_like(position)
            for k, offset in enumerate(offsets):
                device = jnp.where(position // pairs == k, (place ^ offset) % devices_of_head, device)
            pick = (slot_of_row == device * pairs + position % pairs).astype(BF16)
            result = result + jnp.dot(pick, piece[z], preferred_element_type=F32)
        ordered.append(result.astype(BF16))
        heads.append((place ^ by_piece[0][0]) // devices_of_head)
    for g in range(QUERY_GROUP):
        columns = slice(g * HEAD_SIZE, (g + 1) * HEAD_SIZE)
        weights = []
        for head in heads:
            start = pl.multiple_of((g * KEY_VALUE_HEADS + head) * HEAD_SIZE, HEAD_SIZE)
            weights.append(weight_ref[pl.ds(start, HEAD_SIZE), :])
        total = total + jnp.dot(
            jnp.concatenate([o[:, columns] for o in ordered], axis=1),
            jnp.concatenate(weights, axis=0),
            preferred_element_type=F32,
        )
    return total


def first_half_kernel(pairs, places, slot_ref, weight_ref, *refs):
    out_ref = refs[-1]
    out_ref[...] = project_half(
        pairs, places, slot_ref, refs[:-1], weight_ref, jnp.zeros(out_ref.shape, F32)
    )


def second_half_kernel(pairs, places, slot_ref, weight_ref, half_ref, *refs):
    out_ref = refs[-1]
    out_ref[...] = project_half(pairs, places, slot_ref, refs[:-1], weight_ref, half_ref[...]).astype(BF16)


def passed(array, *after):
    return call(pass_kernel, jax.ShapeDtypeStruct(array.shape, array.dtype), (array, *after))


def swap(array, bit, count):
    return lax.ppermute(array, "wide", [(i, i ^ bit) for i in range(count)])


def body(
    count,
    tokens,
    norm_gain,
    slot_of_row,
    lengths,
    w_query,
    key_projection,
    value_projection,
    output_projection,
    slot_key_cache,
    slot_value_cache,
):
    rows, features = tokens.shape
    pairs = slot_key_cache.shape[0]
    width = w_query.shape[0]
    query_columns = w_query.shape[1]
    held = query_columns // HEAD_SIZE
    devices_of_head = rows // pairs
    bits = [1 << b for b in reversed(range(count.bit_length() - 1))]

    slot_row = slot_of_row.reshape(1, rows)
    scaled = call(
        prepare_kernel,
        jax.ShapeDtypeStruct((rows, features), BF16),
        (tokens, norm_gain, slot_row, w_query),
        far=(0, 1, 2, 3),
        scratch=(
            pltpu.VMEM((rows, features), BF16),
            pltpu.VMEM((features,), BF16),
            pltpu.VMEM((1, rows), jnp.int32),
            pltpu.SemaphoreType.DMA((3,)),
        ),
        read=8 * w_query.size,
    )
    index = np.arange(HEAD_SIZE)
    rate = (ROPE_BASE ** (-(index - index % 2) / HEAD_SIZE)).astype(np.float32)[None, :]
    totals = jax.ShapeDtypeStruct((rows, query_columns), F32)
    shares = jax.ShapeDtypeStruct((rows, key_projection.shape[1]), F32)

    def query(by, pieces, *total):
        blocks = sum(piece.shape[0] for piece in pieces)
        return call(
            functools.partial(query_kernel, tuple(o ^ b for b in by for o in offsets), len(pieces)),
            totals,
            (w_query, *pieces, *total),
            near=range(1 + len(pieces)),
            flops=2 * rows * blocks * features * query_columns,
            read=2 * blocks * features * query_columns,
        )

    *outer, far, near, core = bits
    corners = (far | core, near | core, far | near | core)
    blocks, offsets, key_share = scaled[None], [0], None
    for bit in outer:
        arrived = swap(blocks, bit | core, count)
        if key_share is None:
            key_share, value_share, squares, turns, limits = call(
                functools.partial(share_kernel, pairs),
                (
                    shares,
                    shares,
                    jax.ShapeDtypeStruct((rows, HEAD_SIZE), F32),
                    jax.ShapeDtypeStruct((2, pairs, HEAD_SIZE), F32),
                    jax.ShapeDtypeStruct((pairs, HEAD_SIZE), jnp.int32),
                ),
                (scaled, lengths, jnp.asarray(rate), tokens, slot_row, key_projection, value_projection),
                near=(0,),
                far=(3, 4, 5, 6),
                smem=(1,),
                scratch=(
                    pltpu.VMEM((rows, features), BF16),
                    pltpu.VMEM((1, rows), jnp.int32),
                    pltpu.VMEM(key_projection.shape, BF16),
                    pltpu.VMEM(value_projection.shape, BF16),
                    pltpu.SemaphoreType.DMA((4,)),
                ),
                flops=4 * rows * key_projection.size,
                read=4 * key_projection.size,
            )
        blocks = call(
            join_kernel,
            jax.ShapeDtypeStruct((2 * len(offsets), rows, features), BF16),
            (blocks, arrived, key_share),
        )
        offsets = offsets + [o ^ bit ^ core for o in offsets]
    pieces = {by: swap(blocks, by, count) for by in corners}
    total = query((0, core), (blocks, swap(blocks, core, count)))
    joined = call(
        join_kernel,
        jax.ShapeDtypeStruct((3 * len(offsets), rows, features), BF16),
        (*pieces.values(), total),
    )
    last = swap(joined, core, count)
    total = query(corners, (joined,), total)
    by_last = tuple(by ^ core for by in corners)
    sent = held // KEY_VALUE_HEADS if held % KEY_VALUE_HEADS == 0 else held
    message = call(
        functools.partial(
            message_kernel, tuple(o ^ by for by in by_last for o in offsets), pairs
        ),
        jax.ShapeDtypeStruct((count, pairs * (sent + 3), HEAD_SIZE), F32),
        (w_query, total, key_share, value_share, squares, last),
        near=(0, 5),
        flops=6 * blocks.size * query_columns,
        read=6 * len(offsets) * features * query_columns,
    )

    got = lax.all_to_all(message, "wide", 0, 0, tiled=True)
    if sent == 1 and held % KEY_VALUE_HEADS == 0:
        query_rows = got
    else:
        query_rows = (
            got[:, : pairs * sent].reshape(count, sent, pairs, HEAD_SIZE).reshape(-1, pairs, HEAD_SIZE)
        )
        if held % KEY_VALUE_HEADS:
            head = lax.axis_index("wide") // devices_of_head
            query_rows = lax.dynamic_index_in_dim(
                query_rows.reshape(QUERY_GROUP, KEY_VALUE_HEADS, pairs, HEAD_SIZE), head, 1, False
            )
    cache_bytes = 2 * slot_key_cache.size
    attended = call(
        functools.partial(attend_kernel, pairs, width),
        jax.ShapeDtypeStruct((pairs, QUERY_GROUP * HEAD_SIZE), BF16),
        (limits, turns, query_rows, got, slot_key_cache, slot_value_cache),
        near=(4, 5),
        scratch=(
            pltpu.VMEM(
                ((pairs + 1) // 2, min(pairs, 2) * QUERY_GROUP, slot_key_cache.shape[1]), F32
            ),
            pltpu.VMEM((pairs, QUERY_GROUP * HEAD_SIZE), F32),
        ),
        limit=8 * MIB,
        flops=4 * QUERY_GROUP * slot_key_cache.size,
        read=2 * cache_bytes,
    )

    mine = attended[None]
    offsets = [0]
    for bit in bits:
        if near < bit < devices_of_head:
            mine = jnp.concatenate([mine, swap(mine, bit | core, count)], 1)
            offsets = offsets + [o ^ bit ^ core for o in offsets]
    high, low = bits[0] | core, bits[1]
    mine = jnp.concatenate([mine, swap(mine, high, count)], 0)
    corners = (near | core, low | near | core, low | core)
    pieces = {0: mine} | {by: swap(mine, by, count) for by in corners}

    def with_core(*members):
        both = [(by, pieces[by]) for by in members]
        both += [(by ^ core, swap(pieces[by], core, count)) for by in members]
        places = tuple(
            tuple(tuple(o ^ head ^ by for o in offsets) for by, _ in both) for head in (0, high)
        )
        return places, [piece for _, piece in both]

    columns = output_projection.shape[1]
    places, held_pieces = with_core(0, corners[0])
    half = call(
        functools.partial(first_half_kernel, pairs, places),
        jax.ShapeDtypeStruct((rows, columns), F32),
        (slot_row, output_projection, *held_pieces),
        near=(1,),
    )
    places, held_pieces = with_core(*corners[1:])
    return call(
        functools.partial(second_half_kernel, pairs, places),
        jax.ShapeDtypeStruct((rows, columns), BF16),
        (slot_row, output_projection, half, *held_pieces),
        near=(1,),
        flops=rows * output_projection.size,
        read=output_projection.size,
    )


def solution(mesh):
    placed = (
        P("groups", "wide"),
        P("wide"),
        P("groups"),
        P("groups"),
        P(None, "wide"),
        P("wide", None),
        P("wide", None),
        P(None, "wide"),
        P(("groups", "wide"), None, None),
        P(("groups", "wide"), None, None),
    )
    return jax.shard_map(
        functools.partial(body, mesh.shape["wide"]),
        mesh=mesh,
        in_specs=placed,
        out_specs=P("groups", "wide"),
        check_vma=False,
    )
```

```python
import functools
import math

import jax
import jax.numpy as jnp
import numpy as np
from jax import lax
from jax.experimental import pallas as pl
from jax.experimental.pallas import tpu as pltpu
from jax.sharding import PartitionSpec as P

QUERY_HEADS = 64
KEY_VALUE_HEADS = 4
HEAD_SIZE = 128
QUERY_GROUP = QUERY_HEADS // KEY_VALUE_HEADS

EPS = 1e-05
ROPE_BASE = 500000.0
MIB = 1 << 20
F32 = jnp.float32
BF16 = jnp.bfloat16


def call(kernel, out_shape, args, near=(), far=(), smem=(), scratch=(), limit=4 * MIB, flops=0, read=0):
    operands, specs = [], []
    for i, arg in enumerate(args):
        space = pltpu.SMEM if i in smem else pltpu.VMEM
        if i in near:
            arg = pltpu.with_memory_space_constraint(arg, pltpu.VMEM)
        if i in far:
            arg = pltpu.with_memory_space_constraint(arg, pltpu.HBM)
            space = pltpu.HBM
        operands.append(arg)
        specs.append(pl.BlockSpec(memory_space=space))
    return pl.pallas_call(
        kernel,
        out_shape=out_shape,
        in_specs=specs,
        out_specs=jax.tree.map(lambda _: pl.BlockSpec(memory_space=pltpu.VMEM), out_shape),
        scratch_shapes=list(scratch),
        compiler_params=pltpu.CompilerParams(vmem_limit_bytes=limit),
        cost_estimate=pl.CostEstimate(flops=flops, bytes_accessed=read, transcendentals=0),
    )(*operands)


def fetch(pairs, sems):
    copies = [pltpu.make_async_copy(far, near, sems.at[i]) for i, (far, near) in enumerate(pairs)]
    for copy in copies:
        copy.start()
    return copies


def picked_rows(slot_ref):
    rows = slot_ref.shape[1]
    return lax.broadcasted_iota(jnp.int32, (rows, rows), 0) == slot_ref[...]


def prepare_kernel(
    far_tokens, far_gain, far_slot, far_query, scaled_ref, tokens_ref, gain_ref, slot_ref, sems
):
    for copy in fetch(((far_tokens, tokens_ref), (far_gain, gain_ref), (far_slot, slot_ref)), sems):
        copy.wait()
    gain = gain_ref[...].astype(F32).reshape(1, gain_ref.shape[0])
    scaled = (tokens_ref[...].astype(F32) * gain).astype(BF16)
    scaled_ref[...] = jnp.dot(
        picked_rows(slot_ref).astype(BF16), scaled, preferred_element_type=F32
    ).astype(BF16)


def pass_kernel(array_ref, *refs):
    refs[-1][...] = array_ref[...]


def join_kernel(*refs):
    at = 0
    for ref in refs[:-2]:
        refs[-1][at : at + ref.shape[0]] = ref[...]
        at += ref.shape[0]


def share_kernel(
    pairs,
    scaled_ref,
    lengths_ref,
    rate_ref,
    far_tokens,
    far_slot,
    far_key,
    far_value,
    key_share_ref,
    value_share_ref,
    squares_ref,
    turns_ref,
    limits_ref,
    tokens_ref,
    slot_ref,
    key_ref,
    value_ref,
    sems,
):
    copies = fetch(
        ((far_tokens, tokens_ref), (far_slot, slot_ref), (far_key, key_ref), (far_value, value_ref)), sems
    )
    own = (lax.axis_index("wide") * pairs) % lengths_ref.shape[0]
    positions = jnp.concatenate(
        [jnp.full((1, HEAD_SIZE), lengths_ref[own + i], jnp.int32) for i in range(pairs)], 0
    )
    angle = positions.astype(F32) * rate_ref[...]
    turns_ref[0] = jnp.cos(angle)
    turns_ref[1] = jnp.sin(angle)
    limits_ref[...] = positions
    copies[0].wait()
    copies[1].wait()
    rows = tokens_ref.shape[0]
    wide_f = tokens_ref[...].astype(F32)
    squares = jnp.sum(wide_f * wide_f, axis=1, keepdims=True)
    turned = jnp.transpose(jnp.broadcast_to(squares, (rows, rows)))
    squares = jnp.sum(jnp.where(picked_rows(slot_ref), turned, 0.0), axis=1, keepdims=True)
    squares_ref[...] = jnp.broadcast_to(squares, squares_ref.shape)
    copies[2].wait()
    key_share_ref[...] = jnp.dot(scaled_ref[...], key_ref[...], preferred_element_type=F32)
    copies[3].wait()
    value_share_ref[...] = jnp.dot(scaled_ref[...], value_ref[...], preferred_element_type=F32)


def products(offsets, pieces, weight_ref, total):
    place = lax.axis_index("wide")
    blocks = [(ref, k) for ref in pieces for k in range(ref.shape[0])]
    for offset, (ref, k) in zip(offsets, blocks):
        features = ref.shape[2]
        start = pl.multiple_of((place ^ offset) * features, features)
        total = total + jnp.dot(
            ref[k], weight_ref[pl.ds(start, features), :], preferred_element_type=F32
        )
    return total


def query_kernel(offsets, count, weight_ref, *refs):
    pieces, before, out_ref = refs[:count], refs[count:-1], refs[-1]
    total = before[0][...] if before else jnp.zeros(out_ref.shape, F32)
    out_ref[...] = products(offsets, pieces, weight_ref, total)


def turn_kernel(total_ref, keys_ref, turned_ref, same_ref):
    same_ref[...] = total_ref[...]
    pairs, length, _ = keys_ref.shape
    step = math.gcd(length, 512)
    for i in range(pairs):
        for start in range(0, length, step):
            turned_ref[i, :, start : start + step] = jnp.transpose(keys_ref[i, start : start + step, :])


def message_kernel(offsets, pairs, weight_ref, total_ref, key_ref, value_ref, squares_ref, *refs):
    message_ref = refs[-1]
    query = products(offsets, refs[:-1], weight_ref, total_ref[...])
    rows = query.shape[0]
    held = query.shape[1] // HEAD_SIZE
    for target in range(message_ref.shape[0]):
        head, first = target * pairs // rows, target * pairs % rows
        slots = slice(first, first + pairs)
        columns = slice(head * HEAD_SIZE, (head + 1) * HEAD_SIZE)
        sent = range(head, held, KEY_VALUE_HEADS) if held % KEY_VALUE_HEADS == 0 else range(held)
        at = 0
        for j in sent:
            message_ref[target, at : at + pairs, :] = query[slots, j * HEAD_SIZE : (j + 1) * HEAD_SIZE]
            at += pairs
        message_ref[target, at : at + pairs, :] = key_ref[slots, columns]
        message_ref[target, at + pairs : at + 2 * pairs, :] = value_ref[slots, columns]
        message_ref[target, at + 2 * pairs : at + 3 * pairs, :] = squares_ref[slots, :]


def rotated(values, cosines, sines):
    even = lax.broadcasted_iota(jnp.int32, values.shape, 1) % 2 == 0
    swapped = jnp.where(
        even, -pltpu.roll(values, HEAD_SIZE - 1, 1), pltpu.roll(values, 1, 1)
    )
    return values * cosines + swapped * sines


def side_by_side(ref, members, start, size):
    parts = [ref[i, start : start + size, :] for i in members]
    return parts[0] if len(parts) == 1 else jnp.concatenate(parts, axis=1)


def folded(op, array):
    tiles = [array[:, at : at + HEAD_SIZE] for at in range(0, array.shape[1], HEAD_SIZE)]
    while len(tiles) > 1:
        tiles = [op(*tiles[k : k + 2]) if k + 1 < len(tiles) else tiles[k] for k in range(0, len(tiles), 2)]
    return tiles[0]


def attend_kernel(
    pairs, width, limits_ref, turns_ref, query_ref, rest_ref, keys_ref, values_ref, out_ref, scores_ref, wide_ref
):
    group = query_ref.shape[0]
    length = values_ref.shape[1]
    at = rest_ref.shape[1] - 3 * pairs
    summed = jnp.sum(rest_ref[:, at:, :], axis=0)
    score_scale = 1.0 / math.sqrt(HEAD_SIZE)
    step = math.gcd(length, 512)
    many = 2 if pairs % 2 == 0 else 1
    parts = []
    for base in range(0, pairs, many):
        members = range(base, base + many)
        queries, owns, values, limits = [], [], [], []
        for i in members:
            scale = lax.rsqrt(summed[2 * pairs + i : 2 * pairs + i + 1, :] * (1.0 / width) + EPS)
            cosines, sines = turns_ref[0, i : i + 1, :], turns_ref[1, i : i + 1, :]
            query = rotated(query_ref[:, i, :] * scale, cosines, sines).astype(BF16)
            key = jnp.broadcast_to(summed[i : i + 1, :] * scale, (8, HEAD_SIZE))
            key = rotated(key, cosines, sines)[0:1, :].astype(BF16).astype(F32)
            values.append((summed[pairs + i : pairs + i + 1, :] * scale).astype(BF16).astype(F32))
            owns.append(jnp.sum(query.astype(F32) * key, axis=1, keepdims=True))
            limits.append(jnp.broadcast_to(limits_ref[i : i + 1, :], (group, HEAD_SIZE)))
            blank = jnp.zeros_like(query)
            queries.append(
                query
                if many == 1
                else jnp.concatenate([query if j == i else blank for j in members], axis=1)
            )
        stacked = jnp.concatenate(queries, axis=0)
        own = jnp.concatenate(owns, axis=0)
        limit = jnp.concatenate(limits, axis=0)
        column = lax.broadcasted_iota(jnp.int32, (many * group, HEAD_SIZE), 1)
        tops = jnp.broadcast_to(own, (many * group, HEAD_SIZE))
        place = base // many
        for start in range(0, length, step):
            scores = lax.dot_general(
                stacked,
                jnp.concatenate([keys_ref[i, :, start : start + step] for i in members], axis=0),
                (((1,), (0,)), ((), ())),
                preferred_element_type=F32,
            )
            for at in range(0, step, HEAD_SIZE):
                tile = jnp.where(
                    column < limit - (start + at), scores[:, at : at + HEAD_SIZE], -jnp.inf
                )
                scores_ref[place, :, start + at : start + at + HEAD_SIZE] = tile
                tops = jnp.maximum(tops, tile)
        parts.append((members, place, own, tops, values))
    factor = score_scale * math.log2(math.e)
    for members, place, own, tops, values in parts:
        top = jnp.max(tops, axis=1, keepdims=True)
        own_w = jnp.exp2((own - top) * factor)
        sums = jnp.zeros_like(tops)
        blended = jnp.zeros((many * group, many * HEAD_SIZE), F32)
        for start in range(0, length, step):
            weights = jnp.exp2((scores_ref[place, :, start : start + step] - top) * factor)
            sums = sums + folded(jnp.add, weights)
            blended = blended + jnp.dot(
                weights.astype(BF16),
                side_by_side(values_ref, members, start, step),
                preferred_element_type=F32,
            )
        share = 1.0 / (own_w + jnp.sum(sums, axis=1, keepdims=True))
        blended = blended * share
        own_p = (own_w * share).astype(BF16).astype(F32)
        for k, i in enumerate(members):
            rows = slice(k * group, (k + 1) * group)
            result = blended[rows, k * HEAD_SIZE : (k + 1) * HEAD_SIZE] + own_p[rows] * values[k]
            for g in range(group):
                wide_ref[i : i + 1, g * HEAD_SIZE : (g + 1) * HEAD_SIZE] = result[g : g + 1, :]
    out_ref[...] = wide_ref[...].astype(BF16)


def project_half(pairs, places, slot_ref, pieces, weight_ref, total):
    rows = slot_ref.shape[1]
    held = sum(piece.shape[1] for piece in pieces)
    devices_of_head = rows // pairs
    place = lax.axis_index("wide")
    slot_of_row = jnp.transpose(jnp.broadcast_to(slot_ref[...], (rows, rows)))[:, 0:1]
    position = lax.broadcasted_iota(jnp.int32, (rows, held), 1)
    ordered, heads = [], []
    for z, by_piece in enumerate(places):
        device = jnp.zeros_like(position)
        for k, offset in enumerate(o for offsets in by_piece for o in offsets):
            device = jnp.where(position // pairs == k, (place ^ offset) % devices_of_head, device)
        pick = (slot_of_row == device * pairs + position % pairs).astype(BF16)
        result = jnp.dot(
            pick, jnp.concatenate([piece[z].astype(F32) for piece in pieces], axis=0).astype(BF16),
            preferred_element_type=F32
        )
        ordered.append(result.astype(BF16))
        heads.append((place ^ by_piece[0][0]) // devices_of_head)
    for g in range(QUERY_GROUP):
        columns = slice(g * HEAD_SIZE, (g + 1) * HEAD_SIZE)
        weights = []
        for head in heads:
            start = pl.multiple_of((g * KEY_VALUE_HEADS + head) * HEAD_SIZE, HEAD_SIZE)
            weights.append(weight_ref[pl.ds(start, HEAD_SIZE), :])
        total = total + jnp.dot(
            jnp.concatenate([o[:, columns] for o in ordered], axis=1),
            jnp.concatenate(weights, axis=0),
            preferred_element_type=F32,
        )
    return total


def first_half_kernel(pairs, places, slot_ref, weight_ref, *refs):
    out_ref = refs[-1]
    out_ref[...] = project_half(
        pairs, places, slot_ref, refs[:-1], weight_ref, jnp.zeros(out_ref.shape, F32)
    )


def second_half_kernel(pairs, places, slot_ref, weight_ref, half_ref, *refs):
    out_ref = refs[-1]
    out_ref[...] = project_half(pairs, places, slot_ref, refs[:-1], weight_ref, half_ref[...]).astype(BF16)


def passed(array, *after):
    return call(pass_kernel, jax.ShapeDtypeStruct(array.shape, array.dtype), (array, *after))


def swap(array, bit, count):
    return lax.ppermute(array, "wide", [(i, i ^ bit) for i in range(count)])


def body(
    count,
    tokens,
    norm_gain,
    slot_of_row,
    lengths,
    w_query,
    key_projection,
    value_projection,
    output_projection,
    slot_key_cache,
    slot_value_cache,
):
    rows, features = tokens.shape
    pairs = slot_key_cache.shape[0]
    width = w_query.shape[0]
    query_columns = w_query.shape[1]
    held = query_columns // HEAD_SIZE
    devices_of_head = rows // pairs
    bits = [1 << b for b in reversed(range(count.bit_length() - 1))]

    slot_row = slot_of_row.reshape(1, rows)
    scaled = call(
        prepare_kernel,
        jax.ShapeDtypeStruct((rows, features), BF16),
        (tokens, norm_gain, slot_row, w_query),
        far=(0, 1, 2, 3),
        scratch=(
            pltpu.VMEM((rows, features), BF16),
            pltpu.VMEM((features,), BF16),
            pltpu.VMEM((1, rows), jnp.int32),
            pltpu.SemaphoreType.DMA((3,)),
        ),
        read=8 * w_query.size,
    )
    index = np.arange(HEAD_SIZE)
    rate = (ROPE_BASE ** (-(index - index % 2) / HEAD_SIZE)).astype(np.float32)[None, :]
    totals = jax.ShapeDtypeStruct((rows, query_columns), F32)
    shares = jax.ShapeDtypeStruct((rows, key_projection.shape[1]), F32)

    def query(by, pieces, *total):
        blocks = sum(piece.shape[0] for piece in pieces)
        return call(
            functools.partial(query_kernel, tuple(o ^ b for b in by for o in offsets), len(pieces)),
            totals,
            (w_query, *pieces, *total),
            near=range(1 + len(pieces)),
            flops=2 * rows * blocks * features * query_columns,
            read=2 * blocks * features * query_columns,
        )

    *outer, far, near, core = bits
    corners = (far | core, near | core, far | near | core)
    blocks, offsets, key_share = scaled[None], [0], None
    for bit in outer:
        arrived = swap(blocks, bit | core, count)
        if key_share is None:
            key_share, value_share, squares, turns, limits = call(
                functools.partial(share_kernel, pairs),
                (
                    shares,
                    shares,
                    jax.ShapeDtypeStruct((rows, HEAD_SIZE), F32),
                    jax.ShapeDtypeStruct((2, pairs, HEAD_SIZE), F32),
                    jax.ShapeDtypeStruct((pairs, HEAD_SIZE), jnp.int32),
                ),
                (scaled, lengths, jnp.asarray(rate), tokens, slot_row, key_projection, value_projection),
                near=(0,),
                far=(3, 4, 5, 6),
                smem=(1,),
                scratch=(
                    pltpu.VMEM((rows, features), BF16),
                    pltpu.VMEM((1, rows), jnp.int32),
                    pltpu.VMEM(key_projection.shape, BF16),
                    pltpu.VMEM(value_projection.shape, BF16),
                    pltpu.SemaphoreType.DMA((4,)),
                ),
                flops=4 * rows * key_projection.size,
                read=4 * key_projection.size,
            )
        blocks = call(
            join_kernel,
            jax.ShapeDtypeStruct((2 * len(offsets), rows, features), BF16),
            (blocks, arrived, key_share),
        )
        offsets = offsets + [o ^ bit ^ core for o in offsets]
    pieces = {by: swap(blocks, by, count) for by in corners}
    total = query((0, core), (blocks, swap(blocks, core, count)))
    keys, total = call(
        turn_kernel,
        (pltpu.VMEM((pairs, HEAD_SIZE, slot_key_cache.shape[1]), BF16), totals),
        (total, slot_key_cache),
        near=(1,),
        read=2 * slot_key_cache.size,
    )
    joined = call(
        join_kernel,
        jax.ShapeDtypeStruct((3 * len(offsets), rows, features), BF16),
        (*pieces.values(), total),
    )
    last = swap(joined, core, count)
    total = query(corners, (joined,), total)
    by_last = tuple(by ^ core for by in corners)
    sent = held // KEY_VALUE_HEADS if held % KEY_VALUE_HEADS == 0 else held
    message = call(
        functools.partial(
            message_kernel, tuple(o ^ by for by in by_last for o in offsets), pairs
        ),
        jax.ShapeDtypeStruct((count, pairs * (sent + 3), HEAD_SIZE), F32),
        (w_query, total, key_share, value_share, squares, last),
        near=(0, 5),
        flops=6 * blocks.size * query_columns,
        read=6 * len(offsets) * features * query_columns,
    )

    got = lax.all_to_all(message, "wide", 0, 0, tiled=True)
    if sent == 1 and held % KEY_VALUE_HEADS == 0:
        query_rows = got
    else:
        query_rows = (
            got[:, : pairs * sent].reshape(count, sent, pairs, HEAD_SIZE).reshape(-1, pairs, HEAD_SIZE)
        )
        if held % KEY_VALUE_HEADS:
            head = lax.axis_index("wide") // devices_of_head
            query_rows = lax.dynamic_index_in_dim(
                query_rows.reshape(QUERY_GROUP, KEY_VALUE_HEADS, pairs, HEAD_SIZE), head, 1, False
            )
    cache_bytes = 2 * slot_key_cache.size
    attended = call(
        functools.partial(attend_kernel, pairs, width),
        jax.ShapeDtypeStruct((pairs, QUERY_GROUP * HEAD_SIZE), BF16),
        (limits, turns, query_rows, got, keys, slot_value_cache),
        near=(4, 5),
        scratch=(
            pltpu.VMEM(
                ((pairs + 1) // 2, min(pairs, 2) * QUERY_GROUP, slot_key_cache.shape[1]), F32
            ),
            pltpu.VMEM((pairs, QUERY_GROUP * HEAD_SIZE), F32),
        ),
        limit=8 * MIB,
        flops=4 * QUERY_GROUP * slot_key_cache.size,
        read=2 * cache_bytes,
    )

    mine = attended[None]
    offsets = [0]
    for bit in bits:
        if near < bit < devices_of_head:
            mine = jnp.concatenate([mine, swap(mine, bit | core, count)], 1)
            offsets = offsets + [o ^ bit ^ core for o in offsets]
    high, low = bits[0] | core, bits[1]
    mine = jnp.concatenate([mine, swap(mine, high, count)], 0)
    corners = (near | core, low | near | core, low | core)
    pieces = {0: mine} | {by: swap(mine, by, count) for by in corners}

    def with_core(*members):
        both = [(by, pieces[by]) for by in members]
        both += [(by ^ core, swap(pieces[by], core, count)) for by in members]
        places = tuple(
            tuple(tuple(o ^ head ^ by for o in offsets) for by, _ in both) for head in (0, high)
        )
        return places, [piece for _, piece in both]

    columns = output_projection.shape[1]
    places, held_pieces = with_core(0, corners[0])
    half = call(
        functools.partial(first_half_kernel, pairs, places),
        jax.ShapeDtypeStruct((rows, columns), F32),
        (slot_row, output_projection, *held_pieces),
        near=(1,),
    )
    places, held_pieces = with_core(*corners[1:])
    return call(
        functools.partial(second_half_kernel, pairs, places),
        jax.ShapeDtypeStruct((rows, columns), BF16),
        (slot_row, output_projection, half, *held_pieces),
        near=(1,),
        flops=rows * output_projection.size,
        read=output_projection.size,
    )


def solution(mesh):
    placed = (
        P("groups", "wide"),
        P("wide"),
        P("groups"),
        P("groups"),
        P(None, "wide"),
        P("wide", None),
        P("wide", None),
        P(None, "wide"),
        P(("groups", "wide"), None, None),
        P(("groups", "wide"), None, None),
    )
    return jax.shard_map(
        functools.partial(body, mesh.shape["wide"]),
        mesh=mesh,
        in_specs=placed,
        out_specs=P("groups", "wide"),
        check_vma=False,
    )
```

```python
import functools
import math

import jax
import jax.numpy as jnp
import numpy as np
from jax import lax
from jax.experimental import pallas as pl
from jax.experimental.pallas import tpu as pltpu
from jax.sharding import PartitionSpec as P

QUERY_HEADS = 64
KEY_VALUE_HEADS = 4
HEAD_SIZE = 128
QUERY_GROUP = QUERY_HEADS // KEY_VALUE_HEADS

EPS = 1e-05
ROPE_BASE = 500000.0
MIB = 1 << 20
F32 = jnp.float32
BF16 = jnp.bfloat16


def call(kernel, out_shape, args, near=(), far=(), smem=(), scratch=(), limit=4 * MIB, flops=0, read=0):
    operands, specs = [], []
    for i, arg in enumerate(args):
        space = pltpu.SMEM if i in smem else pltpu.VMEM
        if i in near:
            arg = pltpu.with_memory_space_constraint(arg, pltpu.VMEM)
        if i in far:
            arg = pltpu.with_memory_space_constraint(arg, pltpu.HBM)
            space = pltpu.HBM
        operands.append(arg)
        specs.append(pl.BlockSpec(memory_space=space))
    return pl.pallas_call(
        kernel,
        out_shape=out_shape,
        in_specs=specs,
        out_specs=jax.tree.map(lambda _: pl.BlockSpec(memory_space=pltpu.VMEM), out_shape),
        scratch_shapes=list(scratch),
        compiler_params=pltpu.CompilerParams(vmem_limit_bytes=limit),
        cost_estimate=pl.CostEstimate(flops=flops, bytes_accessed=read, transcendentals=0),
    )(*operands)


def fetch(pairs, sems):
    copies = [pltpu.make_async_copy(far, near, sems.at[i]) for i, (far, near) in enumerate(pairs)]
    for copy in copies:
        copy.start()
    return copies


def picked_rows(slot_ref):
    rows = slot_ref.shape[1]
    return lax.broadcasted_iota(jnp.int32, (rows, rows), 0) == slot_ref[...]


def prepare_kernel(
    far_tokens, far_gain, far_slot, far_query, scaled_ref, tokens_ref, gain_ref, slot_ref, sems
):
    for copy in fetch(((far_tokens, tokens_ref), (far_gain, gain_ref), (far_slot, slot_ref)), sems):
        copy.wait()
    gain = gain_ref[...].astype(F32).reshape(1, gain_ref.shape[0])
    scaled = (tokens_ref[...].astype(F32) * gain).astype(BF16)
    scaled_ref[...] = jnp.dot(
        picked_rows(slot_ref).astype(BF16), scaled, preferred_element_type=F32
    ).astype(BF16)


def pass_kernel(array_ref, *refs):
    refs[-1][...] = array_ref[...]


def join_kernel(*refs):
    at = 0
    for ref in refs[:-2]:
        refs[-1][at : at + ref.shape[0]] = ref[...]
        at += ref.shape[0]


def share_kernel(
    pairs,
    scaled_ref,
    lengths_ref,
    rate_ref,
    far_tokens,
    far_slot,
    far_key,
    far_value,
    key_share_ref,
    value_share_ref,
    squares_ref,
    turns_ref,
    limits_ref,
    tokens_ref,
    slot_ref,
    key_ref,
    value_ref,
    sems,
):
    copies = fetch(
        ((far_tokens, tokens_ref), (far_slot, slot_ref), (far_key, key_ref), (far_value, value_ref)), sems
    )
    own = (lax.axis_index("wide") * pairs) % lengths_ref.shape[0]
    positions = jnp.concatenate(
        [jnp.full((1, HEAD_SIZE), lengths_ref[own + i], jnp.int32) for i in range(pairs)], 0
    )
    angle = positions.astype(F32) * rate_ref[...]
    turns_ref[0] = jnp.cos(angle)
    turns_ref[1] = jnp.sin(angle)
    limits_ref[...] = positions
    copies[0].wait()
    copies[1].wait()
    rows = tokens_ref.shape[0]
    wide_f = tokens_ref[...].astype(F32)
    squares = jnp.sum(wide_f * wide_f, axis=1, keepdims=True)
    turned = jnp.transpose(jnp.broadcast_to(squares, (rows, rows)))
    squares = jnp.sum(jnp.where(picked_rows(slot_ref), turned, 0.0), axis=1, keepdims=True)
    squares_ref[...] = jnp.broadcast_to(squares, squares_ref.shape)
    copies[2].wait()
    key_share_ref[...] = jnp.dot(scaled_ref[...], key_ref[...], preferred_element_type=F32)
    copies[3].wait()
    value_share_ref[...] = jnp.dot(scaled_ref[...], value_ref[...], preferred_element_type=F32)


def products(offsets, pieces, weight_ref, total):
    place = lax.axis_index("wide")
    blocks = [(ref, k) for ref in pieces for k in range(ref.shape[0])]
    for offset, (ref, k) in zip(offsets, blocks):
        features = ref.shape[2]
        start = pl.multiple_of((place ^ offset) * features, features)
        total = total + jnp.dot(
            ref[k], weight_ref[pl.ds(start, features), :], preferred_element_type=F32
        )
    return total


def query_kernel(offsets, count, weight_ref, *refs):
    pieces, before, out_ref = refs[:count], refs[count:-1], refs[-1]
    total = before[0][...] if before else jnp.zeros(out_ref.shape, F32)
    out_ref[...] = products(offsets, pieces, weight_ref, total)


def turn_kernel(total_ref, keys_ref, turned_ref, same_ref):
    same_ref[...] = total_ref[...]
    pairs, length, _ = keys_ref.shape
    step = math.gcd(length, 512)
    for i in range(pairs):
        for start in range(0, length, step):
            turned_ref[i, :, start : start + step] = jnp.transpose(keys_ref[i, start : start + step, :])


def halves(array):
    high = array.astype(BF16).astype(F32)
    return [high, array - high]


def message_kernel(offsets, pairs, weight_ref, total_ref, key_ref, value_ref, squares_ref, *refs):
    message_ref = refs[-1]
    query = products(offsets, refs[:-1], weight_ref, total_ref[...])
    rows = query.shape[0]
    held = query.shape[1] // HEAD_SIZE
    lane = lax.broadcasted_iota(jnp.int32, squares_ref.shape, 1) // (HEAD_SIZE // 4)
    left, squares = squares_ref[...], jnp.zeros(squares_ref.shape, F32)
    for k in range(3):
        part = left.astype(BF16).astype(F32)
        squares = jnp.where(lane == k, part, squares)
        left = left - part
    key, value = halves(key_ref[...]), halves(value_ref[...])
    for target in range(message_ref.shape[0]):
        head, first = target * pairs // rows, target * pairs % rows
        slots = slice(first, first + pairs)
        columns = slice(head * HEAD_SIZE, (head + 1) * HEAD_SIZE)
        sent = range(head, held, KEY_VALUE_HEADS) if held % KEY_VALUE_HEADS == 0 else range(held)
        parts = [query[slots, j * HEAD_SIZE : (j + 1) * HEAD_SIZE] for j in sent]
        parts += [half[slots, columns] for half in key + value] + [squares[slots, :]]
        message_ref[target] = jnp.concatenate(parts, axis=0).astype(BF16)


def rotated(values, cosines, sines):
    even = lax.broadcasted_iota(jnp.int32, values.shape, 1) % 2 == 0
    swapped = jnp.where(
        even, -pltpu.roll(values, HEAD_SIZE - 1, 1), pltpu.roll(values, 1, 1)
    )
    return values * cosines + swapped * sines


def side_by_side(ref, members, start, size):
    parts = [ref[i, start : start + size, :] for i in members]
    return parts[0] if len(parts) == 1 else jnp.concatenate(parts, axis=1)


def folded(op, array):
    tiles = [array[:, at : at + HEAD_SIZE] for at in range(0, array.shape[1], HEAD_SIZE)]
    while len(tiles) > 1:
        tiles = [op(*tiles[k : k + 2]) if k + 1 < len(tiles) else tiles[k] for k in range(0, len(tiles), 2)]
    return tiles[0]


def attend_kernel(
    pairs, width, limits_ref, turns_ref, query_ref, rest_ref, keys_ref, values_ref, out_ref, scores_ref, wide_ref, near_ref
):
    group = query_ref.shape[0]
    length = values_ref.shape[1]
    at = rest_ref.shape[1] - 5 * pairs
    near_ref[...] = query_ref[...].astype(F32)
    summed = jnp.sum(rest_ref[...].astype(F32), axis=0)[at:, :]
    new_keys = summed[:pairs, :] + summed[pairs : 2 * pairs, :]
    new_values = summed[2 * pairs : 3 * pairs, :] + summed[3 * pairs : 4 * pairs, :]
    lane = lax.broadcasted_iota(jnp.int32, (pairs, HEAD_SIZE), 1)
    first_of_part = (lane % (HEAD_SIZE // 4) == 0) & (lane < 3 * (HEAD_SIZE // 4))
    squares = jnp.sum(jnp.where(first_of_part, summed[4 * pairs :, :], 0.0), axis=1, keepdims=True)
    score_scale = 1.0 / math.sqrt(HEAD_SIZE)
    step = math.gcd(length, 512)
    many = 2 if pairs % 2 == 0 else 1
    parts = []
    for base in range(0, pairs, many):
        members = range(base, base + many)
        queries, owns, values, limits = [], [], [], []
        for i in members:
            scale = lax.rsqrt(squares[i : i + 1, :] * (1.0 / width) + EPS)
            cosines, sines = turns_ref[0, i : i + 1, :], turns_ref[1, i : i + 1, :]
            query = rotated(near_ref[:, i, :] * scale, cosines, sines).astype(BF16)
            key = jnp.broadcast_to(new_keys[i : i + 1, :] * scale, (8, HEAD_SIZE))
            key = rotated(key, cosines, sines)[0:1, :].astype(BF16).astype(F32)
            values.append((new_values[i : i + 1, :] * scale).astype(BF16).astype(F32))
            owns.append(jnp.sum(query.astype(F32) * key, axis=1, keepdims=True))
            limits.append(jnp.broadcast_to(limits_ref[i : i + 1, :], (group, HEAD_SIZE)))
            blank = jnp.zeros_like(query)
            queries.append(
                query
                if many == 1
                else jnp.concatenate([query if j == i else blank for j in members], axis=1)
            )
        stacked = jnp.concatenate(queries, axis=0)
        own = jnp.concatenate(owns, axis=0)
        limit = jnp.concatenate(limits, axis=0)
        column = lax.broadcasted_iota(jnp.int32, (many * group, HEAD_SIZE), 1)
        tops = jnp.broadcast_to(own, (many * group, HEAD_SIZE))
        place = base // many
        for start in range(0, length, step):
            scores = lax.dot_general(
                stacked,
                jnp.concatenate([keys_ref[i, :, start : start + step] for i in members], axis=0),
                (((1,), (0,)), ((), ())),
                preferred_element_type=F32,
            )
            for at in range(0, step, HEAD_SIZE):
                tile = jnp.where(
                    column < limit - (start + at), scores[:, at : at + HEAD_SIZE], -jnp.inf
                )
                scores_ref[place, :, start + at : start + at + HEAD_SIZE] = tile
                tops = jnp.maximum(tops, tile)
        parts.append((members, place, own, tops, values))
    factor = score_scale * math.log2(math.e)
    for members, place, own, tops, values in parts:
        top = jnp.max(tops, axis=1, keepdims=True)
        own_w = jnp.exp2((own - top) * factor)
        sums = jnp.zeros_like(tops)
        blended = jnp.zeros((many * group, many * HEAD_SIZE), F32)
        for start in range(0, length, step):
            weights = jnp.exp2((scores_ref[place, :, start : start + step] - top) * factor)
            sums = sums + folded(jnp.add, weights)
            blended = blended + jnp.dot(
                weights.astype(BF16),
                side_by_side(values_ref, members, start, step),
                preferred_element_type=F32,
            )
        share = 1.0 / (own_w + jnp.sum(sums, axis=1, keepdims=True))
        blended = blended * share
        own_p = (own_w * share).astype(BF16).astype(F32)
        for k, i in enumerate(members):
            rows = slice(k * group, (k + 1) * group)
            result = blended[rows, k * HEAD_SIZE : (k + 1) * HEAD_SIZE] + own_p[rows] * values[k]
            for g in range(group):
                wide_ref[i : i + 1, g * HEAD_SIZE : (g + 1) * HEAD_SIZE] = result[g : g + 1, :]
    out_ref[...] = wide_ref[...].astype(BF16)


def project_half(pairs, places, slot_ref, pieces, weight_ref, total):
    rows = slot_ref.shape[1]
    held = sum(piece.shape[1] for piece in pieces)
    devices_of_head = rows // pairs
    place = lax.axis_index("wide")
    slot_of_row = jnp.transpose(jnp.broadcast_to(slot_ref[...], (rows, rows)))[:, 0:1]
    position = lax.broadcasted_iota(jnp.int32, (rows, held), 1)
    ordered, heads = [], []
    for z, by_piece in enumerate(places):
        device = jnp.zeros_like(position)
        for k, offset in enumerate(o for offsets in by_piece for o in offsets):
            device = jnp.where(position // pairs == k, (place ^ offset) % devices_of_head, device)
        pick = (slot_of_row == device * pairs + position % pairs).astype(BF16)
        result = jnp.dot(
            pick, jnp.concatenate([piece[z].astype(F32) for piece in pieces], axis=0).astype(BF16),
            preferred_element_type=F32
        )
        ordered.append(result.astype(BF16))
        heads.append((place ^ by_piece[0][0]) // devices_of_head)
    for g in range(QUERY_GROUP):
        columns = slice(g * HEAD_SIZE, (g + 1) * HEAD_SIZE)
        weights = []
        for head in heads:
            start = pl.multiple_of((g * KEY_VALUE_HEADS + head) * HEAD_SIZE, HEAD_SIZE)
            weights.append(weight_ref[pl.ds(start, HEAD_SIZE), :])
        total = total + jnp.dot(
            jnp.concatenate([o[:, columns] for o in ordered], axis=1),
            jnp.concatenate(weights, axis=0),
            preferred_element_type=F32,
        )
    return total


def first_half_kernel(pairs, places, slot_ref, weight_ref, *refs):
    out_ref = refs[-1]
    out_ref[...] = project_half(
        pairs, places, slot_ref, refs[:-1], weight_ref, jnp.zeros(out_ref.shape, F32)
    )


def second_half_kernel(pairs, places, slot_ref, weight_ref, half_ref, *refs):
    out_ref = refs[-1]
    out_ref[...] = project_half(pairs, places, slot_ref, refs[:-1], weight_ref, half_ref[...]).astype(BF16)


def passed(array, *after):
    return call(pass_kernel, jax.ShapeDtypeStruct(array.shape, array.dtype), (array, *after))


def swap(array, bit, count):
    return lax.ppermute(array, "wide", [(i, i ^ bit) for i in range(count)])


def body(
    count,
    tokens,
    norm_gain,
    slot_of_row,
    lengths,
    w_query,
    key_projection,
    value_projection,
    output_projection,
    slot_key_cache,
    slot_value_cache,
):
    rows, features = tokens.shape
    pairs = slot_key_cache.shape[0]
    width = w_query.shape[0]
    query_columns = w_query.shape[1]
    held = query_columns // HEAD_SIZE
    devices_of_head = rows // pairs
    bits = [1 << b for b in reversed(range(count.bit_length() - 1))]

    slot_row = slot_of_row.reshape(1, rows)
    scaled = call(
        prepare_kernel,
        jax.ShapeDtypeStruct((rows, features), BF16),
        (tokens, norm_gain, slot_row, w_query),
        far=(0, 1, 2, 3),
        scratch=(
            pltpu.VMEM((rows, features), BF16),
            pltpu.VMEM((features,), BF16),
            pltpu.VMEM((1, rows), jnp.int32),
            pltpu.SemaphoreType.DMA((3,)),
        ),
        read=8 * w_query.size,
    )
    index = np.arange(HEAD_SIZE)
    rate = (ROPE_BASE ** (-(index - index % 2) / HEAD_SIZE)).astype(np.float32)[None, :]
    totals = jax.ShapeDtypeStruct((rows, query_columns), F32)
    shares = jax.ShapeDtypeStruct((rows, key_projection.shape[1]), F32)

    def query(by, pieces, *total):
        blocks = sum(piece.shape[0] for piece in pieces)
        return call(
            functools.partial(query_kernel, tuple(o ^ b for b in by for o in offsets), len(pieces)),
            totals,
            (w_query, *pieces, *total),
            near=range(1 + len(pieces)),
            flops=2 * rows * blocks * features * query_columns,
            read=2 * blocks * features * query_columns,
        )

    *outer, far, near, core = bits
    corners = (far | core, near | core, far | near | core)
    blocks, offsets, key_share = scaled[None], [0], None
    for bit in outer:
        arrived = swap(blocks, bit | core, count)
        if key_share is None:
            key_share, value_share, squares, turns, limits = call(
                functools.partial(share_kernel, pairs),
                (
                    shares,
                    shares,
                    jax.ShapeDtypeStruct((rows, HEAD_SIZE), F32),
                    jax.ShapeDtypeStruct((2, pairs, HEAD_SIZE), F32),
                    jax.ShapeDtypeStruct((pairs, HEAD_SIZE), jnp.int32),
                ),
                (scaled, lengths, jnp.asarray(rate), tokens, slot_row, key_projection, value_projection),
                near=(0,),
                far=(3, 4, 5, 6),
                smem=(1,),
                scratch=(
                    pltpu.VMEM((rows, features), BF16),
                    pltpu.VMEM((1, rows), jnp.int32),
                    pltpu.VMEM(key_projection.shape, BF16),
                    pltpu.VMEM(value_projection.shape, BF16),
                    pltpu.SemaphoreType.DMA((4,)),
                ),
                flops=4 * rows * key_projection.size,
                read=4 * key_projection.size,
            )
        blocks = call(
            join_kernel,
            jax.ShapeDtypeStruct((2 * len(offsets), rows, features), BF16),
            (blocks, arrived, key_share),
        )
        offsets = offsets + [o ^ bit ^ core for o in offsets]
    pieces = {by: swap(blocks, by, count) for by in corners}
    total = query((0, core), (blocks, swap(blocks, core, count)))
    keys, total = call(
        turn_kernel,
        (pltpu.VMEM((pairs, HEAD_SIZE, slot_key_cache.shape[1]), BF16), totals),
        (total, slot_key_cache),
        near=(1,),
        read=2 * slot_key_cache.size,
    )
    joined = call(
        join_kernel,
        jax.ShapeDtypeStruct((3 * len(offsets), rows, features), BF16),
        (*pieces.values(), total),
    )
    last = swap(joined, core, count)
    total = query(corners, (joined,), total)
    by_last = tuple(by ^ core for by in corners)
    sent = held // KEY_VALUE_HEADS if held % KEY_VALUE_HEADS == 0 else held
    message = call(
        functools.partial(
            message_kernel, tuple(o ^ by for by in by_last for o in offsets), pairs
        ),
        jax.ShapeDtypeStruct((count, pairs * (sent + 5), HEAD_SIZE), BF16),
        (w_query, total, key_share, value_share, squares, last),
        near=(0, 5),
        flops=6 * blocks.size * query_columns,
        read=6 * len(offsets) * features * query_columns,
    )

    got = lax.all_to_all(message, "wide", 0, 0, tiled=True)
    if sent == 1 and held % KEY_VALUE_HEADS == 0:
        query_rows = got
    else:
        query_rows = (
            got[:, : pairs * sent].reshape(count, sent, pairs, HEAD_SIZE).reshape(-1, pairs, HEAD_SIZE)
        )
        if held % KEY_VALUE_HEADS:
            head = lax.axis_index("wide") // devices_of_head
            query_rows = lax.dynamic_index_in_dim(
                query_rows.reshape(QUERY_GROUP, KEY_VALUE_HEADS, pairs, HEAD_SIZE), head, 1, False
            )
    cache_bytes = 2 * slot_key_cache.size
    attended = call(
        functools.partial(attend_kernel, pairs, width),
        jax.ShapeDtypeStruct((pairs, QUERY_GROUP * HEAD_SIZE), BF16),
        (limits, turns, query_rows, got, keys, slot_value_cache),
        near=(4, 5),
        scratch=(
            pltpu.VMEM(
                ((pairs + 1) // 2, min(pairs, 2) * QUERY_GROUP, slot_key_cache.shape[1]), F32
            ),
            pltpu.VMEM((pairs, QUERY_GROUP * HEAD_SIZE), F32),
            pltpu.VMEM(query_rows.shape, F32),
        ),
        limit=8 * MIB,
        flops=4 * QUERY_GROUP * slot_key_cache.size,
        read=2 * cache_bytes,
    )

    mine = attended[None]
    offsets = [0]
    for bit in bits:
        if near < bit < devices_of_head:
            mine = jnp.concatenate([mine, swap(mine, bit | core, count)], 1)
            offsets = offsets + [o ^ bit ^ core for o in offsets]
    high, low = bits[0] | core, bits[1]
    mine = jnp.concatenate([mine, swap(mine, high, count)], 0)
    corners = (near | core, low | near | core, low | core)
    pieces = {0: mine} | {by: swap(mine, by, count) for by in corners}

    def with_core(*members):
        both = [(by, pieces[by]) for by in members]
        both += [(by ^ core, swap(pieces[by], core, count)) for by in members]
        places = tuple(
            tuple(tuple(o ^ head ^ by for o in offsets) for by, _ in both) for head in (0, high)
        )
        return places, [piece for _, piece in both]

    columns = output_projection.shape[1]
    places, held_pieces = with_core(0, corners[0])
    half = call(
        functools.partial(first_half_kernel, pairs, places),
        jax.ShapeDtypeStruct((rows, columns), F32),
        (slot_row, output_projection, *held_pieces),
        near=(1,),
    )
    places, held_pieces = with_core(*corners[1:])
    return call(
        functools.partial(second_half_kernel, pairs, places),
        jax.ShapeDtypeStruct((rows, columns), BF16),
        (slot_row, output_projection, half, *held_pieces),
        near=(1,),
        flops=rows * output_projection.size,
        read=output_projection.size,
    )


def solution(mesh):
    placed = (
        P("groups", "wide"),
        P("wide"),
        P("groups"),
        P("groups"),
        P(None, "wide"),
        P("wide", None),
        P("wide", None),
        P(None, "wide"),
        P(("groups", "wide"), None, None),
        P(("groups", "wide"), None, None),
    )
    return jax.shard_map(
        functools.partial(body, mesh.shape["wide"]),
        mesh=mesh,
        in_specs=placed,
        out_specs=P("groups", "wide"),
        check_vma=False,
    )
```
